1024 devices in a mesh: gx: 16 (over x, y_lo, core), gy: 64 (over z, y_hi).
Axes of the slice: x: 4, y: 4 (y_hi: 2, y_lo: 2; y = y_hi * 2 + y_lo), z: 32, core: 2. Of those that a mesh axis runs over, the one named last changes fastest.
Arguments:
- substrate: float32 [16, 512, 4096], P(None, 'gy', 'gx'), may hold values from 0 to 1
- catalyst: float32 [16, 512, 4096], P(None, 'gy', 'gx'), may hold values from 0 to 1
Outputs:
- substrate_next: float32 [16, 512, 4096], P(None, 'gy', 'gx')
- catalyst_next: float32 [16, 512, 4096], P(None, 'gy', 'gx')
- rebuilt: float32 [2, 16, 4096, 512], P(None, None, ('gx', 'gy'))
The draws below stay inside these ranges and needn't reach their ends.
All inputs are finite; a program needn't handle non-finite values.
Results may differ from the reference program's by a relative error of at most 0.00002.
Values sent between devices are 32-bit elements; how exact they have to be, the bound alone decides.
No kernel may reach another device: no remote copies, remote signals or barrier semaphores. Data moves between devices by JAX's collectives and lax.ppermute only.
A program may use at most 32 MiB of HBM per device.

```python
import jax
import jax.numpy as jnp

Z = 16
NX = 4096
NY = 512


def block_scale(rng, extent, split, low, largest):
    def one(axis_at, shards_of):
        heights = jax.random.uniform(jax.random.fold_in(jax.random.fold_in(rng, 6), axis_at), (shards_of,), jnp.float32, low / len(split), largest / len(split))
        return jnp.repeat(jnp.exp(heights), extent[axis_at] // shards_of).reshape((-1,) + (1,) * (len(extent) - axis_at - 1))

    gain = one(*split[0])
    for cut in split[1:]:
        gain = gain * one(*cut)
    return gain


def setup_inputs(seed: int = 0) -> dict:
    seeds = jax.random.split(jax.random.key(seed), 3)
    return {
        "substrate": jnp.clip(1.0 * jax.random.uniform(seeds[0], (Z, NY, NX), jnp.float32) ** block_scale(seeds[0], (Z, NY, NX), ((1, 64), (2, 16)), -0.2, 0.2), 0.0, 1.0),
        "catalyst": jnp.clip(1.0 * jax.random.uniform(seeds[1], (Z, NY, NX), jnp.float32) ** block_scale(seeds[1], (Z, NY, NX), ((1, 64), (2, 16)), -0.2, 0.2), 0.0, 1.0),
    }


feed_rate = 0.037
kill_rate = 0.06
substrate_diffusion = 0.15
catalyst_diffusion = 0.08


def react(center, spread):
    substrate = center[0]
    catalyst = center[1]
    reaction = substrate * catalyst * catalyst
    new_substrate = substrate + substrate_diffusion * spread[0] - reaction + feed_rate * (1.0 - substrate)
    new_catalyst = catalyst + catalyst_diffusion * spread[1] + reaction - (feed_rate + kill_rate) * catalyst
    return jnp.stack([new_substrate, new_catalyst])


def neighbours(field):
    total = jnp.roll(field, 1, 1) + jnp.roll(field, -1, 1)
    total = total + jnp.roll(field, 1, 2) + jnp.roll(field, -1, 2)
    total = total + jnp.roll(field, 1, 3) + jnp.roll(field, -1, 3)
    return total - 6.0 * field


def restrict(field):
    shape = field.shape
    blocks = field.reshape(shape[0], shape[1], shape[2] // 2, 2, shape[3] // 2, 2)
    return (blocks[:, :, :, 0, :, 0] + blocks[:, :, :, 0, :, 1] + blocks[:, :, :, 1, :, 0] + blocks[:, :, :, 1, :, 1]) * 0.25


def prolong(field):
    return jnp.repeat(jnp.repeat(field, 2, axis=2), 2, axis=3)


def reference(substrate, catalyst):
    state = jnp.stack([substrate, catalyst])
    state = react(state, neighbours(state))
    state = react(state, neighbours(state))
    level1 = restrict(state)
    level2 = restrict(level1)
    coarse = prolong(level2)
    blend = coarse + 0.5 * (level1 - coarse)
    rebuilt = jnp.swapaxes(prolong(blend), 2, 3)
    return state[0], state[1], rebuilt
```

```python
import jax
import jax.numpy as jnp
from jax import lax
from jax.experimental import pallas as pl
from jax.experimental.pallas import tpu as pltpu
from jax.sharding import PartitionSpec as P

feed_rate = 0.037
kill_rate = 0.06
substrate_diffusion = 0.15
catalyst_diffusion = 0.08

planes, cols, rows = 16, 8, 256
owners = 64
f32 = jnp.float32


def lane_ids(shape):
    return lax.broadcasted_iota(jnp.int32, shape, len(shape) - 1)


def slice_kernel(u_ref, v_ref, first_ref, last_ref):
    for f, ref in enumerate((u_ref, v_ref)):
        first_ref[f] = ref[:, 0:2, :]
        last_ref[f] = ref[:, cols - 2 : cols, :]


def edge_kernel(u_ref, v_ref, before_ref, after_ref, edge_ref, pad_ref):
    lane = lane_ids((16, 128))
    low = lane < 64
    here = (lane < 2) | (lane >= 126)
    packed = jnp.zeros((16, 128), f32)
    for f, ref in enumerate((u_ref, v_ref)):
        for p in range(planes):
            q = f * planes + p
            for t, lanes in enumerate((slice(0, 128), slice(rows - 128, rows))):
                pad_ref[q, t, 0:8, :] = ref[p, :, lanes]
                pad_ref[q, t, 8:10, :] = after_ref[f, p, :, lanes]
                pad_ref[q, t, 14:16, :] = before_ref[f, p, :, lanes]
    for q in range(2 * planes):
        both = jnp.where(low, pad_ref[q, 0], pad_ref[q, 1])
        moved = pltpu.roll(jnp.where(here, both, 0.0), 4 * q % 128, 1)
        packed = packed + moved
    row = lax.broadcasted_iota(jnp.int32, (16, 128), 0)
    edge_ref[...] = jnp.where((row < 10) | (row >= 14), packed, 0.0)


def neighbours(x, below, above):
    n, m = x.shape
    total = below + above
    total = total + pltpu.roll(x, 1, 0) + pltpu.roll(x, n - 1, 0)
    total = total + pltpu.roll(x, 1, 1) + pltpu.roll(x, m - 1, 1)
    return total - 6.0 * x


def react(u, v, spread_u, spread_v):
    reaction = u * v * v
    new_u = u + substrate_diffusion * spread_u - reaction + feed_rate * (1.0 - u)
    new_v = v + catalyst_diffusion * spread_v + reaction - (feed_rate + kill_rate) * v
    return new_u, new_v


def step_kernel(
    u_ref, v_ref, before_ref, after_ref, left_ref, right_ref,
    un_ref, vn_ref, send_ref, pad_ref, mid_ref, done_ref, turn_ref,
):
    lane = lane_ids((16, 128))
    beside = jnp.where(lane % 4 < 2, right_ref[...], left_ref[...])
    for f, ref in enumerate((u_ref, v_ref)):
        pad_ref[f, :, 10:14, 0:rows] = jnp.zeros((planes, 4, rows), f32)
        pad_ref[f, :, 0:8, 0:rows] = ref[...]
        pad_ref[f, :, 8:10, 0:rows] = after_ref[f]
        pad_ref[f, :, 14:16, 0:rows] = before_ref[f]
        for p in range(planes):
            q = f * planes + p
            pad_ref[f, p, :, rows : rows + 128] = pltpu.roll(beside, (128 - 4 * q) % 128, 1)

    for p in range(planes):
        below, above = (p - 1) % planes, (p + 1) % planes
        u, v = pad_ref[0, p], pad_ref[1, p]
        spread_u = neighbours(u, pad_ref[0, below], pad_ref[0, above])
        spread_v = neighbours(v, pad_ref[1, below], pad_ref[1, above])
        new_u, new_v = react(u, v, spread_u, spread_v)
        mid_ref[0, p] = new_u
        mid_ref[1, p] = new_v

    for p in range(planes):
        below, above = (p - 1) % planes, (p + 1) % planes
        u, v = mid_ref[0, p], mid_ref[1, p]
        spread_u = neighbours(u, mid_ref[0, below], mid_ref[0, above])
        spread_v = neighbours(v, mid_ref[1, below], mid_ref[1, above])
        new_u, new_v = react(u, v, spread_u, spread_v)
        for f, (ref, new) in enumerate(((un_ref, new_u), (vn_ref, new_v))):
            ref[p] = new[0:8, 0:rows]
            at = 8 * (f * planes + p)
            for t in range(2):
                done_ref[t, at : at + 8, :] = new[0:8, 128 * t : 128 * t + 128]

    many = 2 * planes
    for t in range(2):
        pairs = []
        for c in range(cols // 2):
            one = done_ref[t, pl.ds(2 * c, many, stride=8), :]
            two = done_ref[t, pl.ds(2 * c + 1, many, stride=8), :]
            pairs.append(one + two)
        turn_ref[128 * t : 128 * t + 128, :] = jnp.concatenate(pairs, axis=0).T
    lane = lane_ids((owners, 128))
    r0 = 0.25 * (turn_ref[pl.ds(0, owners, stride=4), :] + turn_ref[pl.ds(1, owners, stride=4), :])
    r1 = 0.25 * (turn_ref[pl.ds(2, owners, stride=4), :] + turn_ref[pl.ds(3, owners, stride=4), :])
    half = owners // 2
    for c1, out in enumerate((
        jnp.where(lane < 64, r0, pltpu.roll(r1, 64, 1)),
        jnp.where(lane < 64, pltpu.roll(r0, 64, 1), r1),
    )):
        send_ref[pl.ds(c1, half, stride=2), :] = out[half:]
        send_ref[pl.ds(2 * half + c1, half, stride=2), :] = out[:half]


def rebuild_kernel(got_ref, out_ref, wide_ref):
    level1 = got_ref[...]
    total = level1 + pltpu.roll(level1, 64, 1)
    coarse = 0.25 * (total + pltpu.roll(total, 32, 1))
    blend = coarse + 0.5 * (level1 - coarse)
    blend = jnp.concatenate([blend[64:], blend[:64]], axis=0)
    odd = pltpu.roll(blend, 96, 1)
    for d in range(2):
        wide_ref[pl.ds(d, 128, stride=4), :] = blend
        wide_ref[pl.ds(2 + d, 128, stride=4), :] = odd
    for t in range(4):
        turned = wide_ref[128 * t : 128 * t + 128, :].T
        for r in range(2):
            part = turned[64 * r : 64 * r + 32]
            for d in range(2):
                out_ref[pl.ds(4 * t + 2 * r + d, 32, stride=16), :] = part


def call(kernel, out_shape, scratch=()):
    return pl.pallas_call(
        kernel,
        out_shape=out_shape,
        scratch_shapes=[pltpu.VMEM(s, f32) for s in scratch],
        compiler_params=pltpu.CompilerParams(vmem_limit_bytes=32 * 1024 * 1024),
    )


def shape(*dims):
    return jax.ShapeDtypeStruct(dims, f32)


def ring(axis, by):
    size = lax.axis_size(axis)
    return [(i, (i + by) % size) for i in range(size)]


def body(u, v):
    column_halo = shape(2, planes, 2, rows)
    first, last = call(slice_kernel, (column_halo, column_halo))(u, v)
    before = lax.ppermute(last, "gy", ring("gy", 1))
    after = lax.ppermute(first, "gy", ring("gy", -1))
    edge = call(edge_kernel, shape(16, 128), [(2 * planes, 2, 16, 128)])(u, v, before, after)
    left = lax.ppermute(edge, "gx", ring("gx", 1))
    right = lax.ppermute(edge, "gx", ring("gx", -1))
    brick = shape(planes, cols, rows)
    padded = (2, planes, 16, rows + 128)
    un, vn, send = call(
        step_kernel, (brick, brick, shape(128, 128)), [padded, padded, (2, 256, 128), (rows, 128)]
    )(u, v, before, after, left, right)
    order = [(i + owners // 2) % owners for i in range(owners)]
    got = lax.all_to_all(
        send.reshape(owners, 2, 128), "gy", 0, 0, tiled=True, axis_index_groups=[order]
    )
    out = call(rebuild_kernel, shape(512, 128), [(512, 128)])(got.reshape(128, 128))
    out = out.reshape(2, planes, 4, 4, 128).transpose(0, 1, 3, 2, 4).reshape(2, planes, 4, 512)
    return un, vn, out


def solution(mesh):
    in_specs = (P(None, "gy", "gx"), P(None, "gy", "gx"))
    out_specs = (P(None, "gy", "gx"), P(None, "gy", "gx"), P(None, None, ("gx", "gy"), None))
    return jax.shard_map(body, mesh=mesh, in_specs=in_specs, out_specs=out_specs, check_vma=False)
```

```python
import jax
import jax.numpy as jnp
from jax import lax
from jax.experimental import pallas as pl
from jax.experimental.pallas import tpu as pltpu
from jax.sharding import PartitionSpec as P

feed_rate = 0.037
kill_rate = 0.06
substrate_diffusion = 0.15
catalyst_diffusion = 0.08

planes, cols, rows = 16, 8, 256
owners = 64
large = 56 * 1024 * 1024
master = 37
f32 = jnp.float32


def lane_ids(shape):
    return lax.broadcasted_iota(jnp.int32, shape, len(shape) - 1)


def odd(axis):
    return lax.axis_index(axis) % 2 == 1


def slice_kernel(u_hbm, v_hbm, one_ref, two_ref, u_ref, v_ref, sems):
    part = planes // 2
    copies = []
    for f, (src, dst) in enumerate(((u_hbm, u_ref), (v_hbm, v_ref))):
        for h in range(2):
            at = pl.ds(h * part, part)
            copies.append((f, h, pltpu.make_async_copy(src.at[at], dst.at[at], sems.at[f, h])))
    for _, _, copy in copies:
        copy.start()
    second = odd("gy")
    for f, h, copy in copies:
        copy.wait()
        at = slice(h * part, h * part + part)
        ref = (u_ref, v_ref)[f]
        first, last = ref[at, 0:2, :], ref[at, cols - 2 : cols, :]
        one_ref[f, at] = jnp.where(second, first, last)
        two_ref[f, at] = jnp.where(second, last, first)


def edge_kernel(u_ref, v_ref, one_ref, two_ref, edge_ref, pad_ref):
    lane = lane_ids((16, 128))
    low = lane < 64
    here = (lane < 2) | (lane >= 126)
    packed = jnp.zeros((16, 128), f32)
    second = odd("gy")
    for f, ref in enumerate((u_ref, v_ref)):
        for p in range(planes):
            one, two = one_ref[f, p], two_ref[f, p]
            after, before = jnp.where(second, two, one), jnp.where(second, one, two)
            q = f * planes + p
            for t, lanes in enumerate((slice(0, 128), slice(rows - 128, rows))):
                pad_ref[q, t, 0:8, :] = ref[p, :, lanes]
                pad_ref[q, t, 8:10, :] = after[:, lanes]
                pad_ref[q, t, 14:16, :] = before[:, lanes]
    for q in range(2 * planes):
        both = jnp.where(low, pad_ref[q, 0], pad_ref[q, 1])
        moved = pltpu.roll(jnp.where(here, both, 0.0), 4 * q % 128, 1)
        packed = packed + moved
    row = lax.broadcasted_iota(jnp.int32, (16, 128), 0)
    edge_ref[...] = jnp.where((row < 10) | (row >= 14), packed, 0.0)


def neighbours(x, below, above):
    n, m = x.shape
    total = below + above
    total = total + pltpu.roll(x, 1, 0) + pltpu.roll(x, n - 1, 0)
    total = total + pltpu.roll(x, 1, 1) + pltpu.roll(x, m - 1, 1)
    return total - 6.0 * x


def react(u, v, spread_u, spread_v):
    reaction = u * v * v
    new_u = u + substrate_diffusion * spread_u - reaction + feed_rate * (1.0 - u)
    new_v = v + catalyst_diffusion * spread_v + reaction - (feed_rate + kill_rate) * v
    return new_u, new_v


def step_kernel(
    u_ref, v_ref, one_ref, two_ref, near_ref, far_ref,
    un_ref, vn_ref, send_ref, pad_ref, mid_ref, done_ref, turn_ref,
):
    right = lane_ids((16, 128)) % 4 < 2
    beside = jnp.where(right != odd("gx"), near_ref[...], far_ref[...])
    second = odd("gy")
    for f, ref in enumerate((u_ref, v_ref)):
        pad_ref[f, :, 10:14, 0:rows] = jnp.zeros((planes, 4, rows), f32)
        pad_ref[f, :, 0:8, 0:rows] = ref[...]
        one, two = one_ref[f], two_ref[f]
        pad_ref[f, :, 8:10, 0:rows] = jnp.where(second, two, one)
        pad_ref[f, :, 14:16, 0:rows] = jnp.where(second, one, two)
        for p in range(planes):
            q = f * planes + p
            pad_ref[f, p, :, rows : rows + 128] = pltpu.roll(beside, (128 - 4 * q) % 128, 1)

    for p in range(planes):
        below, above = (p - 1) % planes, (p + 1) % planes
        u, v = pad_ref[0, p], pad_ref[1, p]
        spread_u = neighbours(u, pad_ref[0, below], pad_ref[0, above])
        spread_v = neighbours(v, pad_ref[1, below], pad_ref[1, above])
        new_u, new_v = react(u, v, spread_u, spread_v)
        mid_ref[0, p] = new_u
        mid_ref[1, p] = new_v

    for p in range(planes):
        below, above = (p - 1) % planes, (p + 1) % planes
        u, v = mid_ref[0, p], mid_ref[1, p]
        spread_u = neighbours(u, mid_ref[0, below], mid_ref[0, above])
        spread_v = neighbours(v, mid_ref[1, below], mid_ref[1, above])
        new_u, new_v = react(u, v, spread_u, spread_v)
        for f, (ref, new) in enumerate(((un_ref, new_u), (vn_ref, new_v))):
            ref[p] = new[0:8, 0:rows]
            at = 8 * (f * planes + p)
            for t in range(2):
                done_ref[t, at : at + 8, :] = new[0:8, 128 * t : 128 * t + 128]

    many = 2 * planes
    for t in range(2):
        pairs = []
        for c in range(cols // 2):
            one = done_ref[t, pl.ds(2 * c, many, stride=8), :]
            two = done_ref[t, pl.ds(2 * c + 1, many, stride=8), :]
            pairs.append(one + two)
        turn_ref[128 * t : 128 * t + 128, :] = jnp.concatenate(pairs, axis=0).T
    lane = lane_ids((owners, 128))
    r0 = 0.25 * (turn_ref[pl.ds(0, owners, stride=4), :] + turn_ref[pl.ds(1, owners, stride=4), :])
    r1 = 0.25 * (turn_ref[pl.ds(2, owners, stride=4), :] + turn_ref[pl.ds(3, owners, stride=4), :])
    for c1, out in enumerate((
        jnp.where(lane < 64, r0, pltpu.roll(r1, 64, 1)),
        jnp.where(lane < 64, pltpu.roll(r0, 64, 1), r1),
    )):
        turn_ref[c1 * owners : c1 * owners + owners, :] = out
    rest = owners - master
    for c1 in range(2):
        at = c1 * owners
        send_ref[pl.ds(c1, rest, stride=2), :] = turn_ref[at + master : at + owners, :]
        send_ref[pl.ds(2 * rest + c1, master, stride=2), :] = turn_ref[at : at + master, :]


def rebuild_kernel(got_ref, out_ref, wide_ref):
    level1 = pltpu.roll(got_ref[...], 2 * master, 0)
    total = level1 + pltpu.roll(level1, 64, 1)
    coarse = 0.25 * (total + pltpu.roll(total, 32, 1))
    blend = coarse + 0.5 * (level1 - coarse)
    shifted = pltpu.roll(blend, 96, 1)
    for d in range(2):
        wide_ref[pl.ds(d, 128, stride=4), :] = blend
        wide_ref[pl.ds(2 + d, 128, stride=4), :] = shifted
    for t in range(4):
        turned = wide_ref[128 * t : 128 * t + 128, :].T
        for r in range(2):
            part = turned[64 * r : 64 * r + 32]
            for d in range(2):
                out_ref[pl.ds(4 * t + 2 * r + d, 32, stride=16), :] = part


def call(kernel, out_shape, scratch=(), sems=(), limit=32 * 1024 * 1024, **kw):
    return pl.pallas_call(
        kernel,
        out_shape=out_shape,
        scratch_shapes=[pltpu.VMEM(s, f32) for s in scratch] + [pltpu.SemaphoreType.DMA(s) for s in sems],
        compiler_params=pltpu.CompilerParams(vmem_limit_bytes=limit),
        **kw,
    )


def shape(*dims):
    return jax.ShapeDtypeStruct(dims, f32)


def pairs(axis, first):
    size = lax.axis_size(axis)
    found = [(i % size, (i + 1) % size) for i in range(first, size, 2)]
    return found + [(j, i) for i, j in found]


def body(u, v):
    brick = shape(planes, cols, rows)
    halo = pltpu.VMEM((2, planes, 2, rows), f32)
    one, two = call(
        slice_kernel, (halo, halo), [(planes, cols, rows)] * 2, [(2, 2)], limit=large,
        in_specs=[pl.BlockSpec(memory_space=pltpu.HBM)] * 2,
    )(u, v)
    two = lax.ppermute(two, "gy", pairs("gy", 1))
    one = lax.ppermute(one, "gy", pairs("gy", 0))
    edge = call(edge_kernel, shape(16, 128), [(2 * planes, 2, 16, 128)])(u, v, one, two)
    far = lax.ppermute(edge, "gx", pairs("gx", 1))
    near = lax.ppermute(edge, "gx", pairs("gx", 0))
    inside = pltpu.VMEM((planes, cols, rows), f32)
    padded = (2, planes, 16, rows + 128)
    un, vn, send = call(
        step_kernel, (brick, brick, shape(128, 128)), [padded, padded, (2, 256, 128), (rows, 128)]
    )(u, v, one, two, near, far)
    order = [(i + master) % owners for i in range(owners)]
    got = lax.all_to_all(
        send.reshape(owners, 2, 128), "gy", 0, 0, tiled=True, axis_index_groups=[order]
    )
    out = call(rebuild_kernel, shape(512, 128), [(512, 128)])(got.reshape(128, 128))
    out = out.reshape(2, planes, 4, 4, 128).transpose(0, 1, 3, 2, 4).reshape(2, planes, 4, 512)
    return un, vn, out


def solution(mesh):
    in_specs = (P(None, "gy", "gx"), P(None, "gy", "gx"))
    out_specs = (P(None, "gy", "gx"), P(None, "gy", "gx"), P(None, None, ("gx", "gy"), None))
    return jax.shard_map(body, mesh=mesh, in_specs=in_specs, out_specs=out_specs, check_vma=False)
```

```python
import jax
import jax.numpy as jnp
from jax import lax
from jax.experimental import pallas as pl
from jax.experimental.pallas import tpu as pltpu
from jax.sharding import PartitionSpec as P

feed_rate = 0.037
kill_rate = 0.06
substrate_diffusion = 0.15
catalyst_diffusion = 0.08

planes, cols, rows = 16, 8, 256
owners = 64
large = 56 * 1024 * 1024
master = 37
f32 = jnp.float32


def lane_ids(shape):
    return lax.broadcasted_iota(jnp.int32, shape, len(shape) - 1)


def odd(axis):
    return lax.axis_index(axis) % 2 == 1


def slice_kernel(u_hbm, v_hbm, first_ref, u_ref, v_ref, sems):
    part, some = planes // 2, pl.ds(0, 4)
    copies = []
    for f, (src, dst) in enumerate(((u_hbm, u_ref), (v_hbm, v_ref))):
        for h in range(2):
            at = pl.ds(h * part, part)
            copy = pltpu.make_async_copy(src.at[at, some], dst.at[at, some], sems.at[f, h])
            copy.start()
            copies.append((f, h, copy))
    for f, h, copy in copies:
        copy.wait()
        at = slice(h * part, h * part + part)
        first_ref[f, at] = (u_ref, v_ref)[f][at, 0:4, :]


def edge_kernel(u_ref, v_ref, next_ref, edge_ref, pad_ref):
    lane = lane_ids((16, 128))
    low = lane < 64
    here = (lane < 2) | (lane >= 126)
    packed = jnp.zeros((16, 128), f32)
    for f, ref in enumerate((u_ref, v_ref)):
        for p in range(planes):
            q = f * planes + p
            for t, lanes in enumerate((slice(0, 128), slice(rows - 128, rows))):
                pad_ref[q, t, 0:6, :] = ref[p, 2:8, lanes]
                pad_ref[q, t, 6:10, :] = next_ref[f, p, :, lanes]
                pad_ref[q, t, 14:16, :] = ref[p, 0:2, lanes]
    for q in range(2 * planes):
        both = jnp.where(low, pad_ref[q, 0], pad_ref[q, 1])
        moved = pltpu.roll(jnp.where(here, both, 0.0), 4 * q % 128, 1)
        packed = packed + moved
    row = lax.broadcasted_iota(jnp.int32, (16, 128), 0)
    edge_ref[...] = jnp.where((row < 10) | (row >= 14), packed, 0.0)


def neighbours(x, below, above):
    n, m = x.shape
    total = below + above
    total = total + pltpu.roll(x, 1, 0) + pltpu.roll(x, n - 1, 0)
    total = total + pltpu.roll(x, 1, 1) + pltpu.roll(x, m - 1, 1)
    return total - 6.0 * x


def react(u, v, spread_u, spread_v):
    reaction = u * v * v
    new_u = u + substrate_diffusion * spread_u - reaction + feed_rate * (1.0 - u)
    new_v = v + catalyst_diffusion * spread_v + reaction - (feed_rate + kill_rate) * v
    return new_u, new_v


def step_kernel(
    u_ref, v_ref, next_ref, near_ref, far_ref,
    un_ref, vn_ref, back_ref, send_ref, pad_ref, mid_ref, done_ref, turn_ref,
):
    right = lane_ids((16, 128)) % 4 < 2
    beside = jnp.where(right != odd("gx"), near_ref[...], far_ref[...])
    for f, ref in enumerate((u_ref, v_ref)):
        pad_ref[f, :, 10:14, 0:rows] = jnp.zeros((planes, 4, rows), f32)
        pad_ref[f, :, 0:6, 0:rows] = ref[:, 2:8, :]
        pad_ref[f, :, 6:10, 0:rows] = next_ref[f]
        pad_ref[f, :, 14:16, 0:rows] = ref[:, 0:2, :]
        for p in range(planes):
            q = f * planes + p
            pad_ref[f, p, :, rows : rows + 128] = pltpu.roll(beside, (128 - 4 * q) % 128, 1)

    for p in range(planes):
        below, above = (p - 1) % planes, (p + 1) % planes
        u, v = pad_ref[0, p], pad_ref[1, p]
        spread_u = neighbours(u, pad_ref[0, below], pad_ref[0, above])
        spread_v = neighbours(v, pad_ref[1, below], pad_ref[1, above])
        new_u, new_v = react(u, v, spread_u, spread_v)
        mid_ref[0, p] = new_u
        mid_ref[1, p] = new_v

    for p in range(planes):
        below, above = (p - 1) % planes, (p + 1) % planes
        u, v = mid_ref[0, p], mid_ref[1, p]
        spread_u = neighbours(u, mid_ref[0, below], mid_ref[0, above])
        spread_v = neighbours(v, mid_ref[1, below], mid_ref[1, above])
        new_u, new_v = react(u, v, spread_u, spread_v)
        for f, (ref, new) in enumerate(((un_ref, new_u), (vn_ref, new_v))):
            ref[p] = new[0:8, 0:rows]
            back_ref[f, p] = new[6:8, 0:rows]
            at = 8 * (f * planes + p)
            for t in range(2):
                done_ref[t, at : at + 8, :] = new[0:8, 128 * t : 128 * t + 128]

    many = 2 * planes
    for t in range(2):
        pairs = []
        for c in range(cols // 2):
            one = done_ref[t, pl.ds(2 * c, many, stride=8), :]
            two = done_ref[t, pl.ds(2 * c + 1, many, stride=8), :]
            pairs.append(one + two)
        turn_ref[128 * t : 128 * t + 128, :] = jnp.concatenate(pairs, axis=0).T
    lane = lane_ids((owners, 128))
    r0 = 0.25 * (turn_ref[pl.ds(0, owners, stride=4), :] + turn_ref[pl.ds(1, owners, stride=4), :])
    r1 = 0.25 * (turn_ref[pl.ds(2, owners, stride=4), :] + turn_ref[pl.ds(3, owners, stride=4), :])
    for c1, out in enumerate((
        jnp.where(lane < 64, r0, pltpu.roll(r1, 64, 1)),
        jnp.where(lane < 64, pltpu.roll(r0, 64, 1), r1),
    )):
        turn_ref[c1 * owners : c1 * owners + owners, :] = out
    rest = owners - master
    for c1 in range(2):
        at = c1 * owners
        send_ref[pl.ds(c1, rest, stride=2), :] = turn_ref[at + master : at + owners, :]
        send_ref[pl.ds(2 * rest + c1, master, stride=2), :] = turn_ref[at : at + master, :]


def join_kernel(un_ref, vn_ref, back_ref, u_out, v_out):
    for f, (ref, out) in enumerate(((un_ref, u_out), (vn_ref, v_out))):
        out[:, 0:2, :] = back_ref[f]
        out[:, 2:8, :] = ref[:, 0:6, :]


def rebuild_kernel(got_ref, out_ref, wide_ref):
    got = pltpu.roll(got_ref[...], 2 * master, 0)
    even = lane_ids((128, 128)) % 64 < 32
    level1 = jnp.where(even, pltpu.roll(pltpu.roll(got, 1, 0), 96, 1), pltpu.roll(got, 32, 1))
    total = level1 + pltpu.roll(level1, 64, 1)
    coarse = 0.25 * (total + pltpu.roll(total, 32, 1))
    blend = coarse + 0.5 * (level1 - coarse)
    shifted = pltpu.roll(blend, 96, 1)
    for d in range(2):
        wide_ref[pl.ds(d, 128, stride=4), :] = blend
        wide_ref[pl.ds(2 + d, 128, stride=4), :] = shifted
    for t in range(4):
        turned = wide_ref[128 * t : 128 * t + 128, :].T
        for r in range(2):
            part = turned[64 * r : 64 * r + 32]
            for d in range(2):
                out_ref[pl.ds(4 * t + 2 * r + d, 32, stride=16), :] = part


def call(kernel, out_shape, scratch=(), sems=(), limit=32 * 1024 * 1024, **kw):
    return pl.pallas_call(
        kernel,
        out_shape=out_shape,
        scratch_shapes=[pltpu.VMEM(s, f32) for s in scratch] + [pltpu.SemaphoreType.DMA(s) for s in sems],
        compiler_params=pltpu.CompilerParams(vmem_limit_bytes=limit),
        **kw,
    )


def shape(*dims):
    return jax.ShapeDtypeStruct(dims, f32)


def ring(axis, by):
    size = lax.axis_size(axis)
    return [(i, (i + by) % size) for i in range(size)]


def pairs(axis, first):
    size = lax.axis_size(axis)
    found = [(i % size, (i + 1) % size) for i in range(first, size, 2)]
    return found + [(j, i) for i, j in found]


def body(u, v):
    brick = shape(planes, cols, rows)
    inside = pltpu.VMEM((planes, cols, rows), f32)
    first = call(
        slice_kernel, pltpu.VMEM((2, planes, 4, rows), f32), [(planes, cols, rows)] * 2, [(2, 2)],
        limit=large, in_specs=[pl.BlockSpec(memory_space=pltpu.HBM)] * 2,
    )(u, v)
    after = lax.ppermute(first, "gy", ring("gy", -1))
    edge = call(edge_kernel, shape(16, 128), [(2 * planes, 2, 16, 128)])(u, v, after)
    far = lax.ppermute(edge, "gx", pairs("gx", 1))
    near = lax.ppermute(edge, "gx", pairs("gx", 0))
    padded = (2, planes, 16, rows + 128)
    un, vn, back, send = call(
        step_kernel, (inside, inside, shape(2, planes, 2, rows), shape(128, 128)),
        [padded, padded, (2, 256, 128), (rows, 128)],
    )(u, v, after, near, far)
    back = lax.ppermute(back, "gy", ring("gy", 1))
    un, vn = call(join_kernel, (brick, brick))(un, vn, back)
    order = [(i + master) % owners for i in range(owners)]
    got = lax.all_to_all(
        send.reshape(owners, 2, 128), "gy", 0, 0, tiled=True, axis_index_groups=[order]
    )
    out = call(rebuild_kernel, shape(512, 128), [(512, 128)])(got.reshape(128, 128))
    out = out.reshape(2, planes, 4, 4, 128).transpose(0, 1, 3, 2, 4).reshape(2, planes, 4, 512)
    return un, vn, out


def solution(mesh):
    in_specs = (P(None, "gy", "gx"), P(None, "gy", "gx"))
    out_specs = (P(None, "gy", "gx"), P(None, "gy", "gx"), P(None, None, ("gx", "gy"), None))
    return jax.shard_map(body, mesh=mesh, in_specs=in_specs, out_specs=out_specs, check_vma=False)
```

```python
import jax
import jax.numpy as jnp
from jax import lax
from jax.experimental import pallas as pl
from jax.experimental.pallas import tpu as pltpu
from jax.sharding import PartitionSpec as P

feed_rate = 0.037
kill_rate = 0.06
substrate_diffusion = 0.15
catalyst_diffusion = 0.08

planes, cols, rows = 16, 8, 256
owners = 64
large = 56 * 1024 * 1024
master = 43
f32 = jnp.float32


def lane_ids(shape):
    return lax.broadcasted_iota(jnp.int32, shape, len(shape) - 1)


def odd(axis):
    return lax.axis_index(axis) % 2 == 1


def slice_kernel(u_hbm, v_hbm, first_ref, u_ref, v_ref, sems):
    part, some = planes // 2, pl.ds(0, 4)
    copies = []
    for f, (src, dst) in enumerate(((u_hbm, u_ref), (v_hbm, v_ref))):
        for h in range(2):
            at = pl.ds(h * part, part)
            copy = pltpu.make_async_copy(src.at[at, some], dst.at[at, some], sems.at[f, h])
            copy.start()
            copies.append((f, h, copy))
    for f, h, copy in copies:
        copy.wait()
        at = slice(h * part, h * part + part)
        first_ref[f, at] = (u_ref, v_ref)[f][at, 0:4, :]


def edge_kernel(u_ref, v_ref, next_ref, edge_ref, pad_ref):
    lane = lane_ids((16, 128))
    low = lane < 64
    here = (lane < 2) | (lane >= 126)
    packed = jnp.zeros((16, 128), f32)
    for f, ref in enumerate((u_ref, v_ref)):
        for p in range(planes):
            q = f * planes + p
            for t, lanes in enumerate((slice(0, 128), slice(rows - 128, rows))):
                pad_ref[q, t, 0:6, :] = ref[p, 2:8, lanes]
                pad_ref[q, t, 6:10, :] = next_ref[f, p, :, lanes]
                pad_ref[q, t, 14:16, :] = ref[p, 0:2, lanes]
    for q in range(2 * planes):
        both = jnp.where(low, pad_ref[q, 0], pad_ref[q, 1])
        moved = pltpu.roll(jnp.where(here, both, 0.0), 4 * q % 128, 1)
        packed = packed + moved
    row = lax.broadcasted_iota(jnp.int32, (16, 128), 0)
    edge_ref[...] = jnp.where((row < 10) | (row >= 14), packed, 0.0)


def neighbours(x, below, above):
    n, m = x.shape
    total = below + above
    total = total + pltpu.roll(x, 1, 0) + pltpu.roll(x, n - 1, 0)
    total = total + pltpu.roll(x, 1, 1) + pltpu.roll(x, m - 1, 1)
    return total - 6.0 * x


def react(u, v, spread_u, spread_v):
    reaction = u * v * v
    new_u = u + substrate_diffusion * spread_u - reaction + feed_rate * (1.0 - u)
    new_v = v + catalyst_diffusion * spread_v + reaction - (feed_rate + kill_rate) * v
    return new_u, new_v


def step_kernel(
    u_ref, v_ref, next_ref, near_ref, far_ref,
    un_ref, vn_ref, back_ref, send_ref, pad_ref, mid_ref, done_ref, turn_ref,
):
    right = lane_ids((16, 128)) % 4 < 2
    beside = jnp.where(right != odd("gx"), near_ref[...], far_ref[...])
    for f, ref in enumerate((u_ref, v_ref)):
        pad_ref[f, :, 10:14, 0:rows] = jnp.zeros((planes, 4, rows), f32)
        pad_ref[f, :, 0:6, 0:rows] = ref[:, 2:8, :]
        pad_ref[f, :, 6:10, 0:rows] = next_ref[f]
        pad_ref[f, :, 14:16, 0:rows] = ref[:, 0:2, :]
        for p in range(planes):
            q = f * planes + p
            pad_ref[f, p, :, rows : rows + 128] = pltpu.roll(beside, (128 - 4 * q) % 128, 1)

    for p in range(planes):
        below, above = (p - 1) % planes, (p + 1) % planes
        u, v = pad_ref[0, p], pad_ref[1, p]
        spread_u = neighbours(u, pad_ref[0, below], pad_ref[0, above])
        spread_v = neighbours(v, pad_ref[1, below], pad_ref[1, above])
        new_u, new_v = react(u, v, spread_u, spread_v)
        mid_ref[0, p] = new_u
        mid_ref[1, p] = new_v

    for p in range(planes):
        below, above = (p - 1) % planes, (p + 1) % planes
        u, v = mid_ref[0, p], mid_ref[1, p]
        spread_u = neighbours(u, mid_ref[0, below], mid_ref[0, above])
        spread_v = neighbours(v, mid_ref[1, below], mid_ref[1, above])
        new_u, new_v = react(u, v, spread_u, spread_v)
        for f, (ref, new) in enumerate(((un_ref, new_u), (vn_ref, new_v))):
            ref[p] = new[0:8, 0:rows]
            back_ref[f, p] = new[6:8, 0:rows]
            at = 8 * (f * planes + p)
            for t in range(2):
                done_ref[t, at : at + 8, :] = new[0:8, 128 * t : 128 * t + 128]

    many = 2 * planes
    for t in range(2):
        pairs = []
        for c in range(cols // 2):
            one = done_ref[t, pl.ds(2 * c, many, stride=8), :]
            two = done_ref[t, pl.ds(2 * c + 1, many, stride=8), :]
            pairs.append(one + two)
        turn_ref[128 * t : 128 * t + 128, :] = jnp.concatenate(pairs, axis=0).T
    lane = lane_ids((owners, 128))
    r0 = 0.25 * (turn_ref[pl.ds(0, owners, stride=4), :] + turn_ref[pl.ds(1, owners, stride=4), :])
    r1 = 0.25 * (turn_ref[pl.ds(2, owners, stride=4), :] + turn_ref[pl.ds(3, owners, stride=4), :])
    for c1, out in enumerate((
        jnp.where(lane < 64, r0, pltpu.roll(r1, 64, 1)),
        jnp.where(lane < 64, pltpu.roll(r0, 64, 1), r1),
    )):
        turn_ref[c1 * owners : c1 * owners + owners, :] = out
    rest = owners - master
    for c1 in range(2):
        at = c1 * owners
        send_ref[pl.ds(c1, rest, stride=2), :] = turn_ref[at + master : at + owners, :]
        send_ref[pl.ds(2 * rest + c1, master, stride=2), :] = turn_ref[at : at + master, :]


def join_kernel(un_ref, vn_ref, back_ref, u_out, v_out):
    for f, (ref, out) in enumerate(((un_ref, u_out), (vn_ref, v_out))):
        out[:, 0:2, :] = back_ref[f]
        out[:, 2:8, :] = ref[:, 0:6, :]


def rebuild_kernel(got_ref, out_ref, wide_ref):
    got = pltpu.roll(got_ref[...], 2 * master, 0)
    even = lane_ids((128, 128)) % 64 < 32
    level1 = jnp.where(even, pltpu.roll(pltpu.roll(got, 1, 0), 96, 1), pltpu.roll(got, 32, 1))
    total = level1 + pltpu.roll(level1, 64, 1)
    coarse = 0.25 * (total + pltpu.roll(total, 32, 1))
    blend = coarse + 0.5 * (level1 - coarse)
    shifted = pltpu.roll(blend, 96, 1)
    for d in range(2):
        wide_ref[pl.ds(d, 128, stride=4), :] = blend
        wide_ref[pl.ds(2 + d, 128, stride=4), :] = shifted
    for t in range(4):
        turned = wide_ref[128 * t : 128 * t + 128, :].T
        for r in range(2):
            part = turned[64 * r : 64 * r + 32]
            for d in range(2):
                out_ref[pl.ds(4 * t + 2 * r + d, 32, stride=16), :] = part


def call(kernel, out_shape, scratch=(), sems=(), limit=32 * 1024 * 1024, **kw):
    return pl.pallas_call(
        kernel,
        out_shape=out_shape,
        scratch_shapes=[pltpu.VMEM(s, f32) for s in scratch] + [pltpu.SemaphoreType.DMA(s) for s in sems],
        compiler_params=pltpu.CompilerParams(vmem_limit_bytes=limit),
        **kw,
    )


def shape(*dims):
    return jax.ShapeDtypeStruct(dims, f32)


def ring(axis, by):
    size = lax.axis_size(axis)
    return [(i, (i + by) % size) for i in range(size)]


def pairs(axis, first):
    size = lax.axis_size(axis)
    found = [(i % size, (i + 1) % size) for i in range(first, size, 2)]
    return found + [(j, i) for i, j in found]


def body(u, v):
    brick = shape(planes, cols, rows)
    inside = pltpu.VMEM((planes, cols, rows), f32)
    first = call(
        slice_kernel, pltpu.VMEM((2, planes, 4, rows), f32), [(planes, cols, rows)] * 2, [(2, 2)],
        limit=large, in_specs=[pl.BlockSpec(memory_space=pltpu.HBM)] * 2,
    )(u, v)
    after = lax.ppermute(first, "gy", ring("gy", -1))
    edge = call(edge_kernel, shape(16, 128), [(2 * planes, 2, 16, 128)])(u, v, after)
    far = lax.ppermute(edge, "gx", pairs("gx", 1))
    near = lax.ppermute(edge, "gx", pairs("gx", 0))
    padded = (2, planes, 16, rows + 128)
    un, vn, back, send = call(
        step_kernel, (inside, inside, shape(2, planes, 2, rows), shape(128, 128)),
        [padded, padded, (2, 256, 128), (rows, 128)],
    )(u, v, after, near, far)
    back = lax.ppermute(back, "gy", ring("gy", 1))
    un, vn = call(join_kernel, (brick, brick))(un, vn, back)
    order = [(i + master) % owners for i in range(owners)]
    got = lax.all_to_all(
        send.reshape(owners, 2, 128), "gy", 0, 0, tiled=True, axis_index_groups=[order]
    )
    out = call(rebuild_kernel, shape(512, 128), [(512, 128)])(got.reshape(128, 128))
    out = out.reshape(2, planes, 4, 4, 128).transpose(0, 1, 3, 2, 4).reshape(2, planes, 4, 512)
    return un, vn, out


def solution(mesh):
    in_specs = (P(None, "gy", "gx"), P(None, "gy", "gx"))
    out_specs = (P(None, "gy", "gx"), P(None, "gy", "gx"), P(None, None, ("gx", "gy"), None))
    return jax.shard_map(body, mesh=mesh, in_specs=in_specs, out_specs=out_specs, check_vma=False)
```

```python
import jax
import jax.numpy as jnp
from jax import lax
from jax.experimental import pallas as pl
from jax.experimental.pallas import tpu as pltpu
from jax.sharding import PartitionSpec as P

feed_rate = 0.037
kill_rate = 0.06
substrate_diffusion = 0.15
catalyst_diffusion = 0.08

planes, cols, rows = 16, 8, 256
owners = 64
large = 56 * 1024 * 1024
master = 43
f32 = jnp.float32


def lane_ids(shape):
    return lax.broadcasted_iota(jnp.int32, shape, len(shape) - 1)


def odd(axis):
    return lax.axis_index(axis) % 2 == 1


def slice_kernel(u_hbm, v_hbm, first_ref, u_ref, v_ref, sems):
    part, some = planes // 2, pl.ds(0, 4)
    copies = []
    for f, (src, dst) in enumerate(((u_hbm, u_ref), (v_hbm, v_ref))):
        for h in range(2):
            at = pl.ds(h * part, part)
            copy = pltpu.make_async_copy(src.at[at, some], dst.at[at, some], sems.at[f, h])
            copy.start()
            copies.append((f, h, copy))
    for f, h, copy in copies:
        copy.wait()
        at = slice(h * part, h * part + part)
        first_ref[f, at] = (u_ref, v_ref)[f][at, 0:4, :]


def edge_kernel(u_ref, v_ref, next_ref, edge_ref, pad_ref):
    lane = lane_ids((16, 128))
    low = lane < 64
    here = (lane < 2) | (lane >= 126)
    packed = jnp.zeros((16, 128), f32)
    for f, ref in enumerate((u_ref, v_ref)):
        for p in range(planes):
            q = f * planes + p
            for t, lanes in enumerate((slice(0, 128), slice(rows - 128, rows))):
                pad_ref[q, t, 0:6, :] = ref[p, 2:8, lanes]
                pad_ref[q, t, 6:10, :] = next_ref[f, p, :, lanes]
                pad_ref[q, t, 14:16, :] = ref[p, 0:2, lanes]
    for q in range(2 * planes):
        both = jnp.where(low, pad_ref[q, 0], pad_ref[q, 1])
        moved = pltpu.roll(jnp.where(here, both, 0.0), 4 * q % 128, 1)
        packed = packed + moved
    row = lax.broadcasted_iota(jnp.int32, (16, 128), 0)
    edge_ref[...] = jnp.where((row < 10) | (row >= 14), packed, 0.0)


def react(u, v, spread_u, spread_v):
    reaction = u * v * v
    new_u = u + substrate_diffusion * spread_u - reaction + feed_rate * (1.0 - u)
    new_v = v + catalyst_diffusion * spread_v + reaction - (feed_rate + kill_rate) * v
    return new_u, new_v


def inner_kernel(u_ref, v_ref, next_ref, edge_ref, mid_ref, pad_ref):
    del edge_ref
    for f, ref in enumerate((u_ref, v_ref)):
        pad_ref[f, :, 10:14, :] = jnp.zeros((planes, 4, rows), f32)
        pad_ref[f, :, 0:6, :] = ref[:, 2:8, :]
        pad_ref[f, :, 6:10, :] = next_ref[f]
        pad_ref[f, :, 14:16, :] = ref[:, 0:2, :]
    lane = lane_ids((16, rows))
    for p in range(planes):
        spreads = []
        for f in range(2):
            x = pad_ref[f, p]
            total = pad_ref[f, (p - 1) % planes] + pad_ref[f, (p + 1) % planes]
            total = total + pltpu.roll(x, 1, 0) + pltpu.roll(x, 15, 0)
            total = total + jnp.where(lane == 0, 0.0, pltpu.roll(x, 1, 1))
            total = total + jnp.where(lane == rows - 1, 0.0, pltpu.roll(x, rows - 1, 1))
            spreads.append(total - 6.0 * x)
        mid_ref[0, p], mid_ref[1, p] = react(pad_ref[0, p], pad_ref[1, p], *spreads)


def step_kernel(
    mid_ref, edge_ref, near_ref, far_ref,
    un_ref, vn_ref, back_ref, send_ref, full_ref, done_ref, turn_ref,
):
    lane = lane_ids((16, 128))
    edge = edge_ref[...]
    beside = jnp.where((lane % 4 < 2) != odd("gx"), near_ref[...], far_ref[...])

    place = (lane + 2) % 64
    total = jnp.where(place < 4, pltpu.roll(beside, 68, 1), pltpu.roll(beside, 4, 1))
    total = total + jnp.where(place >= 60, pltpu.roll(beside, 60, 1), pltpu.roll(beside, 124, 1))
    total = total + pltpu.roll(beside, 1, 0) + pltpu.roll(beside, 15, 0)
    total = total + jnp.where(
        lane % 4 == 3,
        pltpu.roll(beside, 1, 1) + pltpu.roll(edge, 127, 1),
        pltpu.roll(edge, 1, 1) + pltpu.roll(beside, 127, 1),
    )
    spread = total - 6.0 * beside
    other = pltpu.roll(beside, 64, 1)
    first = (lane + 2) % 128 < 64
    outer = react(jnp.where(first, beside, other), jnp.where(first, other, beside), spread, spread)
    outer = jnp.where(first, *outer)

    for f, rate in enumerate((substrate_diffusion, catalyst_diffusion)):
        for p in range(planes):
            q = f * planes + p
            left = jnp.where(lane == 0, pltpu.roll(beside, (1 - 4 * q) % 128, 1), 0.0)
            right = jnp.where(lane == 127, pltpu.roll(beside, (127 - 4 * q) % 128, 1), 0.0)
            full_ref[f, p, :, 0:128] = mid_ref[f, p, :, 0:128] + rate * left
            full_ref[f, p, :, 128:256] = mid_ref[f, p, :, 128:256] + rate * right

    outer = outer[0:8]
    lane = lane_ids((8, rows))
    for p in range(planes):
        spreads = []
        for f in range(2):
            q = f * planes + p
            x = full_ref[f, p]
            total = full_ref[f, (p - 1) % planes, 0:8, :] + full_ref[f, (p + 1) % planes, 0:8, :]
            total = total + pltpu.roll(x, 1, 0)[0:8] + pltpu.roll(x, 15, 0)[0:8]
            x = x[0:8]
            left = pltpu.roll(outer, (1 - 4 * q) % 128, 1)
            right = pltpu.roll(outer, (127 - 4 * q) % 128, 1)
            ends = jnp.concatenate([left, right], axis=1)
            total = total + jnp.where(lane == 0, ends, pltpu.roll(x, 1, 1))
            total = total + jnp.where(lane == rows - 1, ends, pltpu.roll(x, rows - 1, 1))
            spreads.append(total - 6.0 * x)
        news = react(full_ref[0, p, 0:8, :], full_ref[1, p, 0:8, :], *spreads)
        for f, (ref, new) in enumerate(zip((un_ref, vn_ref), news)):
            ref[p] = new
            back_ref[f, p] = new[6:8]
            at = 8 * (f * planes + p)
            for t in range(2):
                done_ref[t, at : at + 8, :] = new[:, 128 * t : 128 * t + 128]

    many = 2 * planes
    for t in range(2):
        pairs = []
        for c in range(cols // 2):
            one = done_ref[t, pl.ds(2 * c, many, stride=8), :]
            two = done_ref[t, pl.ds(2 * c + 1, many, stride=8), :]
            pairs.append(one + two)
        turn_ref[128 * t : 128 * t + 128, :] = jnp.concatenate(pairs, axis=0).T
    lane = lane_ids((owners, 128))
    r0 = 0.25 * (turn_ref[pl.ds(0, owners, stride=4), :] + turn_ref[pl.ds(1, owners, stride=4), :])
    r1 = 0.25 * (turn_ref[pl.ds(2, owners, stride=4), :] + turn_ref[pl.ds(3, owners, stride=4), :])
    for c1, out in enumerate((
        jnp.where(lane < 64, r0, pltpu.roll(r1, 64, 1)),
        jnp.where(lane < 64, pltpu.roll(r0, 64, 1), r1),
    )):
        turn_ref[c1 * owners : c1 * owners + owners, :] = out
    rest = owners - master
    for c1 in range(2):
        at = c1 * owners
        send_ref[pl.ds(c1, rest, stride=2), :] = turn_ref[at + master : at + owners, :]
        send_ref[pl.ds(2 * rest + c1, master, stride=2), :] = turn_ref[at : at + master, :]


def join_kernel(un_ref, vn_ref, back_ref, u_out, v_out):
    for f, (ref, out) in enumerate(((un_ref, u_out), (vn_ref, v_out))):
        out[:, 0:2, :] = back_ref[f]
        out[:, 2:8, :] = ref[:, 0:6, :]


def rebuild_kernel(got_ref, out_ref, wide_ref):
    got = pltpu.roll(got_ref[...], 2 * master, 0)
    even = lane_ids((128, 128)) % 64 < 32
    level1 = jnp.where(even, pltpu.roll(pltpu.roll(got, 1, 0), 96, 1), pltpu.roll(got, 32, 1))
    total = level1 + pltpu.roll(level1, 64, 1)
    coarse = 0.25 * (total + pltpu.roll(total, 32, 1))
    blend = coarse + 0.5 * (level1 - coarse)
    shifted = pltpu.roll(blend, 96, 1)
    for d in range(2):
        wide_ref[pl.ds(d, 128, stride=4), :] = blend
        wide_ref[pl.ds(2 + d, 128, stride=4), :] = shifted
    for t in range(4):
        turned = wide_ref[128 * t : 128 * t + 128, :].T
        for r in range(2):
            part = turned[64 * r : 64 * r + 32]
            for d in range(2):
                out_ref[pl.ds(4 * t + 2 * r + d, 32, stride=16), :] = part


def call(kernel, out_shape, scratch=(), sems=(), limit=32 * 1024 * 1024, **kw):
    return pl.pallas_call(
        kernel,
        out_shape=out_shape,
        scratch_shapes=[pltpu.VMEM(s, f32) for s in scratch] + [pltpu.SemaphoreType.DMA(s) for s in sems],
        compiler_params=pltpu.CompilerParams(vmem_limit_bytes=limit),
        **kw,
    )


def shape(*dims):
    return jax.ShapeDtypeStruct(dims, f32)


def ring(axis, by):
    size = lax.axis_size(axis)
    return [(i, (i + by) % size) for i in range(size)]


def pairs(axis, first):
    size = lax.axis_size(axis)
    found = [(i % size, (i + 1) % size) for i in range(first, size, 2)]
    return found + [(j, i) for i, j in found]


def body(u, v):
    brick = shape(planes, cols, rows)
    inside = pltpu.VMEM((planes, cols, rows), f32)
    first = call(
        slice_kernel, pltpu.VMEM((2, planes, 4, rows), f32), [(planes, cols, rows)] * 2, [(2, 2)],
        limit=large, in_specs=[pl.BlockSpec(memory_space=pltpu.HBM)] * 2,
    )(u, v)
    after = lax.ppermute(first, "gy", ring("gy", -1))
    edge = call(edge_kernel, shape(16, 128), [(2 * planes, 2, 16, 128)])(u, v, after)
    far = lax.ppermute(edge, "gx", pairs("gx", 1))
    near = lax.ppermute(edge, "gx", pairs("gx", 0))
    padded = (2, planes, 16, rows)
    mid = call(inner_kernel, pltpu.VMEM(padded, f32), [padded])(u, v, after, edge)
    un, vn, back, send = call(
        step_kernel, (inside, inside, shape(2, planes, 2, rows), shape(128, 128)),
        [padded, (2, 256, 128), (rows, 128)],
    )(mid, edge, near, far)
    back = lax.ppermute(back, "gy", ring("gy", 1))
    un, vn = call(join_kernel, (brick, brick))(un, vn, back)
    order = [(i + master) % owners for i in range(owners)]
    got = lax.all_to_all(
        send.reshape(owners, 2, 128), "gy", 0, 0, tiled=True, axis_index_groups=[order]
    )
    out = call(rebuild_kernel, shape(512, 128), [(512, 128)])(got.reshape(128, 128))
    out = out.reshape(2, planes, 4, 4, 128).transpose(0, 1, 3, 2, 4).reshape(2, planes, 4, 512)
    return un, vn, out


def solution(mesh):
    in_specs = (P(None, "gy", "gx"), P(None, "gy", "gx"))
    out_specs = (P(None, "gy", "gx"), P(None, "gy", "gx"), P(None, None, ("gx", "gy"), None))
    return jax.shard_map(body, mesh=mesh, in_specs=in_specs, out_specs=out_specs, check_vma=False)
```

```python
import jax
import jax.numpy as jnp
from jax import lax
from jax.experimental import pallas as pl
from jax.experimental.pallas import tpu as pltpu
from jax.sharding import PartitionSpec as P

feed_rate = 0.037
kill_rate = 0.06
substrate_diffusion = 0.15
catalyst_diffusion = 0.08

planes, cols, rows = 16, 8, 256
owners = 64
large = 56 * 1024 * 1024
master = 43
f32 = jnp.float32


def lane_ids(shape):
    return lax.broadcasted_iota(jnp.int32, shape, len(shape) - 1)


def odd(axis):
    return lax.axis_index(axis) % 2 == 1


def slice_kernel(u_hbm, v_hbm, first_ref, u_ref, v_ref, sems):
    part, some = planes // 2, pl.ds(0, 4)
    copies = []
    for f, (src, dst) in enumerate(((u_hbm, u_ref), (v_hbm, v_ref))):
        for h in range(2):
            at = pl.ds(h * part, part)
            copy = pltpu.make_async_copy(src.at[at, some], dst.at[at, some], sems.at[f, h])
            copy.start()
            copies.append((f, h, copy))
    for f, h, copy in copies:
        copy.wait()
        at = slice(h * part, h * part + part)
        first_ref[f, at] = (u_ref, v_ref)[f][at, 0:4, :]


def fetch_kernel(u_hbm, v_hbm, first_ref, u_ref, v_ref, sems):
    del first_ref
    copies = [
        pltpu.make_async_copy(src, dst, sems.at[f])
        for f, (src, dst) in enumerate(((u_hbm, u_ref), (v_hbm, v_ref)))
    ]
    for copy in copies:
        copy.start()
    for copy in copies:
        copy.wait()


def edge_kernel(u_ref, v_ref, next_ref, edge_ref, pad_ref):
    lane = lane_ids((16, 128))
    low = lane < 64
    here = (lane < 2) | (lane >= 126)
    packed = jnp.zeros((16, 128), f32)
    for f, ref in enumerate((u_ref, v_ref)):
        for p in range(planes):
            q = f * planes + p
            for t, lanes in enumerate((slice(0, 128), slice(rows - 128, rows))):
                pad_ref[q, t, 0:6, :] = ref[p, 2:8, lanes]
                pad_ref[q, t, 6:10, :] = next_ref[f, p, :, lanes]
                pad_ref[q, t, 14:16, :] = ref[p, 0:2, lanes]
    for q in range(2 * planes):
        both = jnp.where(low, pad_ref[q, 0], pad_ref[q, 1])
        moved = pltpu.roll(jnp.where(here, both, 0.0), 4 * q % 128, 1)
        packed = packed + moved
    row = lax.broadcasted_iota(jnp.int32, (16, 128), 0)
    edge_ref[...] = jnp.where((row < 10) | (row >= 14), packed, 0.0)


def react(u, v, spread_u, spread_v):
    reaction = u * v * v
    new_u = u + substrate_diffusion * spread_u - reaction + feed_rate * (1.0 - u)
    new_v = v + catalyst_diffusion * spread_v + reaction - (feed_rate + kill_rate) * v
    return new_u, new_v


def inner_kernel(u_ref, v_ref, next_ref, edge_ref, mid_ref, pad_ref):
    del edge_ref
    for f, ref in enumerate((u_ref, v_ref)):
        pad_ref[f, :, 10:14, :] = jnp.zeros((planes, 4, rows), f32)
        pad_ref[f, :, 0:6, :] = ref[:, 2:8, :]
        pad_ref[f, :, 6:10, :] = next_ref[f]
        pad_ref[f, :, 14:16, :] = ref[:, 0:2, :]
    lane = lane_ids((16, rows))
    for p in range(planes):
        spreads = []
        for f in range(2):
            x = pad_ref[f, p]
            total = pad_ref[f, (p - 1) % planes] + pad_ref[f, (p + 1) % planes]
            total = total + pltpu.roll(x, 1, 0) + pltpu.roll(x, 15, 0)
            total = total + jnp.where(lane == 0, 0.0, pltpu.roll(x, 1, 1))
            total = total + jnp.where(lane == rows - 1, 0.0, pltpu.roll(x, rows - 1, 1))
            spreads.append(total - 6.0 * x)
        mid_ref[0, p], mid_ref[1, p] = react(pad_ref[0, p], pad_ref[1, p], *spreads)


def step_kernel(
    mid_ref, edge_ref, near_ref, far_ref,
    un_ref, vn_ref, back_ref, send_ref, full_ref, done_ref, turn_ref,
):
    lane = lane_ids((16, 128))
    edge = edge_ref[...]
    beside = jnp.where((lane % 4 < 2) != odd("gx"), near_ref[...], far_ref[...])

    place = (lane + 2) % 64
    total = jnp.where(place < 4, pltpu.roll(beside, 68, 1), pltpu.roll(beside, 4, 1))
    total = total + jnp.where(place >= 60, pltpu.roll(beside, 60, 1), pltpu.roll(beside, 124, 1))
    total = total + pltpu.roll(beside, 1, 0) + pltpu.roll(beside, 15, 0)
    total = total + jnp.where(
        lane % 4 == 3,
        pltpu.roll(beside, 1, 1) + pltpu.roll(edge, 127, 1),
        pltpu.roll(edge, 1, 1) + pltpu.roll(beside, 127, 1),
    )
    spread = total - 6.0 * beside
    other = pltpu.roll(beside, 64, 1)
    first = (lane + 2) % 128 < 64
    outer = react(jnp.where(first, beside, other), jnp.where(first, other, beside), spread, spread)
    outer = jnp.where(first, *outer)

    def swap(x):
        return jnp.where(lane_ids(x.shape) % 4 == 0, pltpu.roll(x, 1, 1), pltpu.roll(x, 127, 1))

    beside = swap(beside)
    for f, rate in enumerate((substrate_diffusion, catalyst_diffusion)):
        for p in range(planes):
            q = f * planes + p
            ends = pltpu.roll(beside, -4 * q % 128, 1)
            left = jnp.where(lane == 0, ends, 0.0)
            right = jnp.where(lane == 127, ends, 0.0)
            full_ref[f, p, :, 0:128] = mid_ref[f, p, :, 0:128] + rate * left
            full_ref[f, p, :, 128:256] = mid_ref[f, p, :, 128:256] + rate * right

    outer = swap(outer[0:8])
    lane = lane_ids((8, rows))
    for p in range(planes):
        spreads = []
        for f in range(2):
            q = f * planes + p
            x = full_ref[f, p]
            total = full_ref[f, (p - 1) % planes, 0:8, :] + full_ref[f, (p + 1) % planes, 0:8, :]
            total = total + pltpu.roll(x, 1, 0)[0:8] + pltpu.roll(x, 15, 0)[0:8]
            x = x[0:8]
            ends = pltpu.roll(outer, -4 * q % 128, 1)
            ends = jnp.concatenate([ends, ends], axis=1)
            total = total + jnp.where(lane == 0, ends, pltpu.roll(x, 1, 1))
            total = total + jnp.where(lane == rows - 1, ends, pltpu.roll(x, rows - 1, 1))
            spreads.append(total - 6.0 * x)
        news = react(full_ref[0, p, 0:8, :], full_ref[1, p, 0:8, :], *spreads)
        for f, (ref, new) in enumerate(zip((un_ref, vn_ref), news)):
            ref[p] = new
            back_ref[f, p] = new[6:8]
            at = 8 * (f * planes + p)
            for t in range(2):
                done_ref[t, at : at + 8, :] = new[:, 128 * t : 128 * t + 128]

    many = 2 * planes
    for t in range(2):
        pairs = []
        for c in range(cols // 2):
            one = done_ref[t, pl.ds(2 * c, many, stride=8), :]
            two = done_ref[t, pl.ds(2 * c + 1, many, stride=8), :]
            pairs.append(one + two)
        turn_ref[128 * t : 128 * t + 128, :] = jnp.concatenate(pairs, axis=0).T
    lane = lane_ids((owners, 128))
    r0 = 0.25 * (turn_ref[pl.ds(0, owners, stride=4), :] + turn_ref[pl.ds(1, owners, stride=4), :])
    r1 = 0.25 * (turn_ref[pl.ds(2, owners, stride=4), :] + turn_ref[pl.ds(3, owners, stride=4), :])
    for c1, out in enumerate((
        jnp.where(lane < 64, r0, pltpu.roll(r1, 64, 1)),
        jnp.where(lane < 64, pltpu.roll(r0, 64, 1), r1),
    )):
        turn_ref[c1 * owners : c1 * owners + owners, :] = out
    rest = owners - master
    for c1 in range(2):
        at = c1 * owners
        send_ref[pl.ds(c1, rest, stride=2), :] = turn_ref[at + master : at + owners, :]
        send_ref[pl.ds(2 * rest + c1, master, stride=2), :] = turn_ref[at : at + master, :]


def join_kernel(un_ref, vn_ref, back_ref, u_out, v_out):
    for f, (ref, out) in enumerate(((un_ref, u_out), (vn_ref, v_out))):
        out[:, 0:2, :] = back_ref[f]
        out[:, 2:8, :] = ref[:, 0:6, :]


def rebuild_kernel(got_ref, out_ref, wide_ref):
    got = pltpu.roll(got_ref[...], 2 * master, 0)
    even = lane_ids((128, 128)) % 64 < 32
    level1 = jnp.where(even, pltpu.roll(pltpu.roll(got, 1, 0), 96, 1), pltpu.roll(got, 32, 1))
    total = level1 + pltpu.roll(level1, 64, 1)
    coarse = 0.25 * (total + pltpu.roll(total, 32, 1))
    blend = coarse + 0.5 * (level1 - coarse)
    shifted = pltpu.roll(blend, 96, 1)
    for d in range(2):
        wide_ref[pl.ds(d, 128, stride=4), :] = blend
        wide_ref[pl.ds(2 + d, 128, stride=4), :] = shifted
    for t in range(4):
        turned = wide_ref[128 * t : 128 * t + 128, :].T
        for r in range(2):
            part = turned[64 * r : 64 * r + 32]
            for d in range(2):
                out_ref[pl.ds(4 * t + 2 * r + d, 32, stride=16), :] = part


def call(kernel, out_shape, scratch=(), sems=(), limit=32 * 1024 * 1024, **kw):
    return pl.pallas_call(
        kernel,
        out_shape=out_shape,
        scratch_shapes=[pltpu.VMEM(s, f32) for s in scratch] + [pltpu.SemaphoreType.DMA(s) for s in sems],
        compiler_params=pltpu.CompilerParams(vmem_limit_bytes=limit),
        **kw,
    )


def shape(*dims):
    return jax.ShapeDtypeStruct(dims, f32)


def ring(axis, by):
    size = lax.axis_size(axis)
    return [(i, (i + by) % size) for i in range(size)]


def pairs(axis, first):
    size = lax.axis_size(axis)
    found = [(i % size, (i + 1) % size) for i in range(first, size, 2)]
    return found + [(j, i) for i, j in found]


def body(u, v):
    brick = shape(planes, cols, rows)
    inside = pltpu.VMEM((planes, cols, rows), f32)
    first = call(
        slice_kernel, pltpu.VMEM((2, planes, 4, rows), f32), [(planes, cols, rows)] * 2, [(2, 2)],
        limit=large, in_specs=[pl.BlockSpec(memory_space=pltpu.HBM)] * 2,
    )(u, v)
    after = lax.ppermute(first, "gy", ring("gy", -1))
    u, v = call(
        fetch_kernel, (inside, inside), sems=[(2,)], limit=large,
        in_specs=[pl.BlockSpec(memory_space=pltpu.HBM)] * 2 + [pl.BlockSpec(memory_space=pltpu.VMEM)],
    )(u, v, first)
    edge = call(edge_kernel, shape(16, 128), [(2 * planes, 2, 16, 128)])(u, v, after)
    far = lax.ppermute(edge, "gx", pairs("gx", 1))
    near = lax.ppermute(edge, "gx", pairs("gx", 0))
    padded = (2, planes, 16, rows)
    mid = call(inner_kernel, pltpu.VMEM(padded, f32), [padded])(u, v, after, edge)
    un, vn, back, send = call(
        step_kernel, (inside, inside, shape(2, planes, 2, rows), shape(128, 128)),
        [padded, (2, 256, 128), (rows, 128)],
    )(mid, edge, near, far)
    back = lax.ppermute(back, "gy", ring("gy", 1))
    un, vn = call(join_kernel, (brick, brick))(un, vn, back)
    order = [(i + master) % owners for i in range(owners)]
    got = lax.all_to_all(
        send.reshape(owners, 2, 128), "gy", 0, 0, tiled=True, axis_index_groups=[order]
    )
    out = call(rebuild_kernel, shape(512, 128), [(512, 128)])(got.reshape(128, 128))
    out = out.reshape(2, planes, 4, 4, 128).transpose(0, 1, 3, 2, 4).reshape(2, planes, 4, 512)
    return un, vn, out


def solution(mesh):
    in_specs = (P(None, "gy", "gx"), P(None, "gy", "gx"))
    out_specs = (P(None, "gy", "gx"), P(None, "gy", "gx"), P(None, None, ("gx", "gy"), None))
    return jax.shard_map(body, mesh=mesh, in_specs=in_specs, out_specs=out_specs, check_vma=False)
```

```python
import jax
import jax.numpy as jnp
from jax import lax
from jax.experimental import pallas as pl
from jax.experimental.pallas import tpu as pltpu
from jax.sharding import PartitionSpec as P

feed_rate = 0.037
kill_rate = 0.06
substrate_diffusion = 0.15
catalyst_diffusion = 0.08

planes, cols, rows = 16, 8, 256
owners = 64
large = 56 * 1024 * 1024
master = 45
f32 = jnp.float32


def lane_ids(shape):
    return lax.broadcasted_iota(jnp.int32, shape, len(shape) - 1)


def odd(axis):
    return lax.axis_index(axis) % 2 == 1


def slice_kernel(u_hbm, v_hbm, first_ref, u_ref, v_ref, sems):
    part, some = planes // 2, pl.ds(0, 4)
    copies = []
    for f, (src, dst) in enumerate(((u_hbm, u_ref), (v_hbm, v_ref))):
        for h in range(2):
            at = pl.ds(h * part, part)
            copy = pltpu.make_async_copy(src.at[at, some], dst.at[at, some], sems.at[f, h])
            copy.start()
            copies.append((f, h, copy))
    for f, h, copy in copies:
        copy.wait()
        at = slice(h * part, h * part + part)
        first_ref[f, at] = (u_ref, v_ref)[f][at, 0:4, :]


def fetch_kernel(u_hbm, v_hbm, first_ref, u_ref, v_ref, sems):
    del first_ref
    copies = [
        pltpu.make_async_copy(src, dst, sems.at[f])
        for f, (src, dst) in enumerate(((u_hbm, u_ref), (v_hbm, v_ref)))
    ]
    for copy in copies:
        copy.start()
    for copy in copies:
        copy.wait()


def edge_kernel(u_ref, v_ref, next_ref, edge_ref, pad_ref):
    lane = lane_ids((16, 128))
    low = lane < 64
    here = (lane < 2) | (lane >= 126)
    packed = jnp.zeros((16, 128), f32)
    for f, ref in enumerate((u_ref, v_ref)):
        for p in range(planes):
            q = f * planes + p
            for t, lanes in enumerate((slice(0, 128), slice(rows - 128, rows))):
                pad_ref[q, t, 0:6, :] = ref[p, 2:8, lanes]
                pad_ref[q, t, 6:10, :] = next_ref[f, p, :, lanes]
                pad_ref[q, t, 14:16, :] = ref[p, 0:2, lanes]
    for q in range(2 * planes):
        both = jnp.where(low, pad_ref[q, 0], pad_ref[q, 1])
        moved = pltpu.roll(jnp.where(here, both, 0.0), 4 * q % 128, 1)
        packed = packed + moved
    row = lax.broadcasted_iota(jnp.int32, (16, 128), 0)
    edge_ref[...] = jnp.where((row < 10) | (row >= 14), packed, 0.0)


def react(u, v, spread_u, spread_v):
    reaction = u * v * v
    new_u = u + substrate_diffusion * spread_u - reaction + feed_rate * (1.0 - u)
    new_v = v + catalyst_diffusion * spread_v + reaction - (feed_rate + kill_rate) * v
    return new_u, new_v


def inner_kernel(u_ref, v_ref, next_ref, edge_ref, mid_ref, pad_ref):
    del edge_ref
    for f, ref in enumerate((u_ref, v_ref)):
        pad_ref[f, :, 10:14, :] = jnp.zeros((planes, 4, rows), f32)
        pad_ref[f, :, 0:6, :] = ref[:, 2:8, :]
        pad_ref[f, :, 6:10, :] = next_ref[f]
        pad_ref[f, :, 14:16, :] = ref[:, 0:2, :]
    lane = lane_ids((16, rows))
    for p in range(planes):
        spreads = []
        for f in range(2):
            x = pad_ref[f, p]
            total = pad_ref[f, (p - 1) % planes] + pad_ref[f, (p + 1) % planes]
            total = total + pltpu.roll(x, 1, 0) + pltpu.roll(x, 15, 0)
            total = total + jnp.where(lane == 0, 0.0, pltpu.roll(x, 1, 1))
            total = total + jnp.where(lane == rows - 1, 0.0, pltpu.roll(x, rows - 1, 1))
            spreads.append(total - 6.0 * x)
        mid_ref[0, p], mid_ref[1, p] = react(pad_ref[0, p], pad_ref[1, p], *spreads)


def step_kernel(
    mid_ref, edge_ref, near_ref, far_ref,
    un_ref, vn_ref, back_ref, send_ref, full_ref, done_ref, turn_ref,
):
    lane = lane_ids((16, 128))
    edge = edge_ref[...]
    beside = jnp.where((lane % 4 < 2) != odd("gx"), near_ref[...], far_ref[...])

    place = (lane + 2) % 64
    total = jnp.where(place < 4, pltpu.roll(beside, 68, 1), pltpu.roll(beside, 4, 1))
    total = total + jnp.where(place >= 60, pltpu.roll(beside, 60, 1), pltpu.roll(beside, 124, 1))
    total = total + pltpu.roll(beside, 1, 0) + pltpu.roll(beside, 15, 0)
    total = total + jnp.where(
        lane % 4 == 3,
        pltpu.roll(beside, 1, 1) + pltpu.roll(edge, 127, 1),
        pltpu.roll(edge, 1, 1) + pltpu.roll(beside, 127, 1),
    )
    spread = total - 6.0 * beside
    other = pltpu.roll(beside, 64, 1)
    first = (lane + 2) % 128 < 64
    outer = react(jnp.where(first, beside, other), jnp.where(first, other, beside), spread, spread)
    outer = jnp.where(first, *outer)

    def swap(x):
        return jnp.where(lane_ids(x.shape) % 4 == 0, pltpu.roll(x, 1, 1), pltpu.roll(x, 127, 1))

    beside = swap(beside)
    for f, rate in enumerate((substrate_diffusion, catalyst_diffusion)):
        for p in range(planes):
            q = f * planes + p
            ends = pltpu.roll(beside, -4 * q % 128, 1)
            left = jnp.where(lane == 0, ends, 0.0)
            right = jnp.where(lane == 127, ends, 0.0)
            full_ref[f, p, :, 0:128] = mid_ref[f, p, :, 0:128] + rate * left
            full_ref[f, p, :, 128:256] = mid_ref[f, p, :, 128:256] + rate * right

    outer = swap(outer[0:8])
    lane = lane_ids((8, rows))
    for p in range(planes):
        spreads = []
        for f in range(2):
            q = f * planes + p
            x = full_ref[f, p]
            total = full_ref[f, (p - 1) % planes, 0:8, :] + full_ref[f, (p + 1) % planes, 0:8, :]
            total = total + pltpu.roll(x, 1, 0)[0:8] + pltpu.roll(x, 15, 0)[0:8]
            x = x[0:8]
            ends = pltpu.roll(outer, -4 * q % 128, 1)
            ends = jnp.concatenate([ends, ends], axis=1)
            total = total + jnp.where(lane == 0, ends, pltpu.roll(x, 1, 1))
            total = total + jnp.where(lane == rows - 1, ends, pltpu.roll(x, rows - 1, 1))
            spreads.append(total - 6.0 * x)
        news = react(full_ref[0, p, 0:8, :], full_ref[1, p, 0:8, :], *spreads)
        for f, (ref, new) in enumerate(zip((un_ref, vn_ref), news)):
            ref[p] = new
            back_ref[f, p] = new[6:8]
            at = 8 * (f * planes + p)
            for t in range(2):
                done_ref[t, at : at + 8, :] = new[:, 128 * t : 128 * t + 128]

    many = 2 * planes
    for t in range(2):
        pairs = []
        for c in range(cols // 2):
            one = done_ref[t, pl.ds(2 * c, many, stride=8), :]
            two = done_ref[t, pl.ds(2 * c + 1, many, stride=8), :]
            pairs.append(one + two)
        turn_ref[128 * t : 128 * t + 128, :] = jnp.concatenate(pairs, axis=0).T
    lane = lane_ids((owners, 128))
    r0 = 0.25 * (turn_ref[pl.ds(0, owners, stride=4), :] + turn_ref[pl.ds(1, owners, stride=4), :])
    r1 = 0.25 * (turn_ref[pl.ds(2, owners, stride=4), :] + turn_ref[pl.ds(3, owners, stride=4), :])
    for c1, out in enumerate((
        jnp.where(lane < 64, r0, pltpu.roll(r1, 64, 1)),
        jnp.where(lane < 64, pltpu.roll(r0, 64, 1), r1),
    )):
        turn_ref[c1 * owners : c1 * owners + owners, :] = out
    rest = owners - master
    for c1 in range(2):
        at = c1 * owners
        send_ref[pl.ds(c1, rest, stride=2), :] = turn_ref[at + master : at + owners, :]
        send_ref[pl.ds(2 * rest + c1, master, stride=2), :] = turn_ref[at : at + master, :]


def join_kernel(un_ref, vn_ref, back_ref, u_out, v_out):
    for f, (ref, out) in enumerate(((un_ref, u_out), (vn_ref, v_out))):
        out[:, 0:2, :] = back_ref[f]
        out[:, 2:8, :] = ref[:, 0:6, :]


def rebuild_kernel(got_ref, out_hbm, wide_ref, out_ref, sems):
    got = pltpu.roll(got_ref[...], 2 * master, 0)
    even = lane_ids((128, 128)) % 64 < 32
    level1 = jnp.where(even, pltpu.roll(pltpu.roll(got, 1, 0), 96, 1), pltpu.roll(got, 32, 1))
    total = level1 + pltpu.roll(level1, 64, 1)
    coarse = 0.25 * (total + pltpu.roll(total, 32, 1))
    blend = coarse + 0.5 * (level1 - coarse)
    shifted = pltpu.roll(blend, 96, 1)
    for d in range(2):
        wide_ref[pl.ds(d, 128, stride=4), :] = blend
        wide_ref[pl.ds(2 + d, 128, stride=4), :] = shifted
    copies = []
    for half in range(2):
        for t in range(2):
            at = 128 * (2 * half + t)
            turned = wide_ref[at : at + 128, :].T
            for r in range(2):
                part = turned[64 * r : 64 * r + 32]
                for d in range(2):
                    out_ref[half, pl.ds(4 * t + 2 * r + d, 32, stride=8), :] = part
        copies.append(pltpu.make_async_copy(
            out_ref.at[half].reshape(32, 8, 128), out_hbm.at[:, pl.ds(8 * half, 8), :], sems.at[half]
        ))
        copies[-1].start()
    for copy in copies:
        copy.wait()


def call(kernel, out_shape, scratch=(), sems=(), limit=32 * 1024 * 1024, **kw):
    return pl.pallas_call(
        kernel,
        out_shape=out_shape,
        scratch_shapes=[pltpu.VMEM(s, f32) for s in scratch] + [pltpu.SemaphoreType.DMA(s) for s in sems],
        compiler_params=pltpu.CompilerParams(vmem_limit_bytes=limit),
        **kw,
    )


def shape(*dims):
    return jax.ShapeDtypeStruct(dims, f32)


def ring(axis, by):
    size = lax.axis_size(axis)
    return [(i, (i + by) % size) for i in range(size)]


def pairs(axis, first):
    size = lax.axis_size(axis)
    found = [(i % size, (i + 1) % size) for i in range(first, size, 2)]
    return found + [(j, i) for i, j in found]


def body(u, v):
    brick = shape(planes, cols, rows)
    inside = pltpu.VMEM((planes, cols, rows), f32)
    first = call(
        slice_kernel, pltpu.VMEM((2, planes, 4, rows), f32), [(planes, cols, rows)] * 2, [(2, 2)],
        limit=large, in_specs=[pl.BlockSpec(memory_space=pltpu.HBM)] * 2,
    )(u, v)
    after = lax.ppermute(first, "gy", ring("gy", -1))
    u, v = call(
        fetch_kernel, (inside, inside), sems=[(2,)], limit=large,
        in_specs=[pl.BlockSpec(memory_space=pltpu.HBM)] * 2 + [pl.BlockSpec(memory_space=pl.ANY)],
    )(u, v, first)
    edge = call(edge_kernel, shape(16, 128), [(2 * planes, 2, 16, 128)])(u, v, after)
    far = lax.ppermute(edge, "gx", pairs("gx", 1))
    near = lax.ppermute(edge, "gx", pairs("gx", 0))
    padded = (2, planes, 16, rows)
    mid = call(inner_kernel, pltpu.VMEM(padded, f32), [padded])(u, v, after, edge)
    un, vn, back, send = call(
        step_kernel, (inside, inside, shape(2, planes, 2, rows), shape(128, 128)),
        [padded, (2, 256, 128), (rows, 128)],
    )(mid, edge, near, far)
    back = lax.ppermute(back, "gy", ring("gy", 1))
    un, vn = call(join_kernel, (brick, brick))(un, vn, back)
    order = [(i + master) % owners for i in range(owners)]
    got = lax.all_to_all(
        send.reshape(owners, 2, 128), "gy", 0, 0, tiled=True, axis_index_groups=[order]
    )
    out = call(
        rebuild_kernel, shape(32, 16, 128), [(512, 128), (2, 256, 128)], [(2,)],
        out_specs=pl.BlockSpec(memory_space=pl.ANY),
    )(got.reshape(128, 128))
    out = out.reshape(2, planes, 4, 4, 128).transpose(0, 1, 3, 2, 4).reshape(2, planes, 4, 512)
    return un, vn, out


def solution(mesh):
    in_specs = (P(None, "gy", "gx"), P(None, "gy", "gx"))
    out_specs = (P(None, "gy", "gx"), P(None, "gy", "gx"), P(None, None, ("gx", "gy"), None))
    return jax.shard_map(body, mesh=mesh, in_specs=in_specs, out_specs=out_specs, check_vma=False)
```

```python
import jax
import jax.numpy as jnp
from jax import lax
from jax.experimental import pallas as pl
from jax.experimental.pallas import tpu as pltpu
from jax.sharding import PartitionSpec as P

feed_rate = 0.037
kill_rate = 0.06
substrate_diffusion = 0.15
catalyst_diffusion = 0.08

planes, cols, rows = 16, 8, 256
owners = 64
large = 56 * 1024 * 1024
master = 45
f32 = jnp.float32


def lane_ids(shape):
    return lax.broadcasted_iota(jnp.int32, shape, len(shape) - 1)


def odd(axis):
    return lax.axis_index(axis) % 2 == 1


def slice_kernel(u_hbm, v_hbm, first_ref, ready_ref, u_ref, v_ref, sems):
    part, some = planes // 2, pl.ds(0, 4)
    copies = []
    for f, (src, dst) in enumerate(((u_hbm, u_ref), (v_hbm, v_ref))):
        for h in range(2):
            at = pl.ds(h * part, part)
            copy = pltpu.make_async_copy(src.at[at, some], dst.at[at, some], sems.at[f, h])
            copy.start()
            copies.append((f, h, copy))
    for f, h, copy in copies:
        copy.wait()
        at = slice(h * part, h * part + part)
        first_ref[f, at] = (u_ref, v_ref)[f][at, 0:4, :]
    ready_ref[...] = first_ref[0, 0, 0:1, 0:128]


def fetch_kernel(u_hbm, v_hbm, ready_ref, u_ref, v_ref, sems):
    del ready_ref
    copies = [
        pltpu.make_async_copy(src, dst, sems.at[f])
        for f, (src, dst) in enumerate(((u_hbm, u_ref), (v_hbm, v_ref)))
    ]
    for copy in copies:
        copy.start()
    for copy in copies:
        copy.wait()


def edge_kernel(u_ref, v_ref, next_ref, edge_ref, pad_ref):
    lane = lane_ids((16, 128))
    low = lane < 64
    here = (lane < 2) | (lane >= 126)
    packed = jnp.zeros((16, 128), f32)
    for f, ref in enumerate((u_ref, v_ref)):
        for p in range(planes):
            q = f * planes + p
            for t, lanes in enumerate((slice(0, 128), slice(rows - 128, rows))):
                pad_ref[q, t, 0:6, :] = ref[p, 2:8, lanes]
                pad_ref[q, t, 6:10, :] = next_ref[f, p, :, lanes]
                pad_ref[q, t, 14:16, :] = ref[p, 0:2, lanes]
    for q in range(2 * planes):
        both = jnp.where(low, pad_ref[q, 0], pad_ref[q, 1])
        moved = pltpu.roll(jnp.where(here, both, 0.0), 4 * q % 128, 1)
        packed = packed + moved
    row = lax.broadcasted_iota(jnp.int32, (16, 128), 0)
    edge_ref[...] = jnp.where((row < 10) | (row >= 14), packed, 0.0)


def react(u, v, spread_u, spread_v):
    reaction = u * v * v
    new_u = u + substrate_diffusion * spread_u - reaction + feed_rate * (1.0 - u)
    new_v = v + catalyst_diffusion * spread_v + reaction - (feed_rate + kill_rate) * v
    return new_u, new_v


def inner_kernel(u_ref, v_ref, next_ref, edge_ref, mid_ref, pad_ref):
    del edge_ref
    for f, ref in enumerate((u_ref, v_ref)):
        pad_ref[f, :, 10:14, :] = jnp.zeros((planes, 4, rows), f32)
        pad_ref[f, :, 0:6, :] = ref[:, 2:8, :]
        pad_ref[f, :, 6:10, :] = next_ref[f]
        pad_ref[f, :, 14:16, :] = ref[:, 0:2, :]
    lane = lane_ids((16, rows))
    for p in range(planes):
        spreads = []
        for f in range(2):
            x = pad_ref[f, p]
            total = pad_ref[f, (p - 1) % planes] + pad_ref[f, (p + 1) % planes]
            total = total + pltpu.roll(x, 1, 0) + pltpu.roll(x, 15, 0)
            total = total + jnp.where(lane == 0, 0.0, pltpu.roll(x, 1, 1))
            total = total + jnp.where(lane == rows - 1, 0.0, pltpu.roll(x, rows - 1, 1))
            spreads.append(total - 6.0 * x)
        mid_ref[0, p], mid_ref[1, p] = react(pad_ref[0, p], pad_ref[1, p], *spreads)


def step_kernel(
    mid_ref, edge_ref, near_ref, far_ref,
    un_ref, vn_ref, back_ref, send_ref, full_ref, done_ref, turn_ref,
):
    lane = lane_ids((16, 128))
    edge = edge_ref[...]
    beside = jnp.where((lane % 4 < 2) != odd("gx"), near_ref[...], far_ref[...])

    place = (lane + 2) % 64
    total = jnp.where(place < 4, pltpu.roll(beside, 68, 1), pltpu.roll(beside, 4, 1))
    total = total + jnp.where(place >= 60, pltpu.roll(beside, 60, 1), pltpu.roll(beside, 124, 1))
    total = total + pltpu.roll(beside, 1, 0) + pltpu.roll(beside, 15, 0)
    total = total + jnp.where(
        lane % 4 == 3,
        pltpu.roll(beside, 1, 1) + pltpu.roll(edge, 127, 1),
        pltpu.roll(edge, 1, 1) + pltpu.roll(beside, 127, 1),
    )
    spread = total - 6.0 * beside
    other = pltpu.roll(beside, 64, 1)
    first = (lane + 2) % 128 < 64
    outer = react(jnp.where(first, beside, other), jnp.where(first, other, beside), spread, spread)
    outer = jnp.where(first, *outer)

    def swap(x):
        return jnp.where(lane_ids(x.shape) % 4 == 0, pltpu.roll(x, 1, 1), pltpu.roll(x, 127, 1))

    beside = swap(beside)
    for f, rate in enumerate((substrate_diffusion, catalyst_diffusion)):
        for p in range(planes):
            q = f * planes + p
            ends = pltpu.roll(beside, -4 * q % 128, 1)
            left = jnp.where(lane == 0, ends, 0.0)
            right = jnp.where(lane == 127, ends, 0.0)
            full_ref[f, p, :, 0:128] = mid_ref[f, p, :, 0:128] + rate * left
            full_ref[f, p, :, 128:256] = mid_ref[f, p, :, 128:256] + rate * right

    outer = swap(outer[0:8])
    lane = lane_ids((8, rows))
    for p in range(planes):
        spreads = []
        for f in range(2):
            q = f * planes + p
            x = full_ref[f, p]
            total = full_ref[f, (p - 1) % planes, 0:8, :] + full_ref[f, (p + 1) % planes, 0:8, :]
            total = total + pltpu.roll(x, 1, 0)[0:8] + pltpu.roll(x, 15, 0)[0:8]
            x = x[0:8]
            ends = pltpu.roll(outer, -4 * q % 128, 1)
            ends = jnp.concatenate([ends, ends], axis=1)
            total = total + jnp.where(lane == 0, ends, pltpu.roll(x, 1, 1))
            total = total + jnp.where(lane == rows - 1, ends, pltpu.roll(x, rows - 1, 1))
            spreads.append(total - 6.0 * x)
        news = react(full_ref[0, p, 0:8, :], full_ref[1, p, 0:8, :], *spreads)
        for f, (ref, new) in enumerate(zip((un_ref, vn_ref), news)):
            ref[p] = new
            back_ref[f, p] = new[6:8]
            at = 8 * (f * planes + p)
            for t in range(2):
                done_ref[t, at : at + 8, :] = new[:, 128 * t : 128 * t + 128]

    many = 2 * planes
    for t in range(2):
        pairs = []
        for c in range(cols // 2):
            one = done_ref[t, pl.ds(2 * c, many, stride=8), :]
            two = done_ref[t, pl.ds(2 * c + 1, many, stride=8), :]
            pairs.append(one + two)
        turn_ref[128 * t : 128 * t + 128, :] = jnp.concatenate(pairs, axis=0).T
    lane = lane_ids((owners, 128))
    r0 = 0.25 * (turn_ref[pl.ds(0, owners, stride=4), :] + turn_ref[pl.ds(1, owners, stride=4), :])
    r1 = 0.25 * (turn_ref[pl.ds(2, owners, stride=4), :] + turn_ref[pl.ds(3, owners, stride=4), :])
    for c1, out in enumerate((
        jnp.where(lane < 64, r0, pltpu.roll(r1, 64, 1)),
        jnp.where(lane < 64, pltpu.roll(r0, 64, 1), r1),
    )):
        turn_ref[c1 * owners : c1 * owners + owners, :] = out
    rest = owners - master
    for c1 in range(2):
        at = c1 * owners
        send_ref[pl.ds(c1, rest, stride=2), :] = turn_ref[at + master : at + owners, :]
        send_ref[pl.ds(2 * rest + c1, master, stride=2), :] = turn_ref[at : at + master, :]


def join_kernel(un_ref, vn_ref, back_ref, u_out, v_out):
    for f, (ref, out) in enumerate(((un_ref, u_out), (vn_ref, v_out))):
        out[:, 0:2, :] = back_ref[f]
        out[:, 2:8, :] = ref[:, 0:6, :]


def rebuild_kernel(got_ref, out_hbm, wide_ref, out_ref, sems):
    got = pltpu.roll(got_ref[...], 2 * master, 0)
    even = lane_ids((128, 128)) % 64 < 32
    level1 = jnp.where(even, pltpu.roll(pltpu.roll(got, 1, 0), 96, 1), pltpu.roll(got, 32, 1))
    total = level1 + pltpu.roll(level1, 64, 1)
    coarse = 0.25 * (total + pltpu.roll(total, 32, 1))
    blend = coarse + 0.5 * (level1 - coarse)
    shifted = pltpu.roll(blend, 96, 1)
    for d in range(2):
        wide_ref[pl.ds(d, 128, stride=4), :] = blend
        wide_ref[pl.ds(2 + d, 128, stride=4), :] = shifted
    copies = []
    for half in range(2):
        for t in range(2):
            at = 128 * (2 * half + t)
            turned = wide_ref[at : at + 128, :].T
            for r in range(2):
                part = turned[64 * r : 64 * r + 32]
                for d in range(2):
                    out_ref[half, pl.ds(4 * t + 2 * r + d, 32, stride=8), :] = part
        copies.append(pltpu.make_async_copy(
            out_ref.at[half].reshape(32, 8, 128), out_hbm.at[:, pl.ds(8 * half, 8), :], sems.at[half]
        ))
        copies[-1].start()
    for copy in copies:
        copy.wait()


def call(kernel, out_shape, scratch=(), sems=(), limit=32 * 1024 * 1024, **kw):
    return pl.pallas_call(
        kernel,
        out_shape=out_shape,
        scratch_shapes=[pltpu.VMEM(s, f32) for s in scratch] + [pltpu.SemaphoreType.DMA(s) for s in sems],
        compiler_params=pltpu.CompilerParams(vmem_limit_bytes=limit),
        **kw,
    )


def shape(*dims):
    return jax.ShapeDtypeStruct(dims, f32)


def ring(axis, by):
    size = lax.axis_size(axis)
    return [(i, (i + by) % size) for i in range(size)]


def pairs(axis, first):
    size = lax.axis_size(axis)
    found = [(i % size, (i + 1) % size) for i in range(first, size, 2)]
    return found + [(j, i) for i, j in found]


def body(u, v):
    brick = shape(planes, cols, rows)
    inside = pltpu.VMEM((planes, cols, rows), f32)
    first, ready = call(
        slice_kernel, (pltpu.VMEM((2, planes, 4, rows), f32), shape(1, 128)), [(planes, cols, rows)] * 2, [(2, 2)],
        limit=large, in_specs=[pl.BlockSpec(memory_space=pltpu.HBM)] * 2,
    )(u, v)
    after = lax.ppermute(first, "gy", ring("gy", -1))
    u, v = call(
        fetch_kernel, (inside, inside), sems=[(2,)], limit=large,
        in_specs=[pl.BlockSpec(memory_space=pltpu.HBM)] * 2 + [pl.BlockSpec(memory_space=pl.ANY)],
    )(u, v, ready)
    edge = call(edge_kernel, shape(16, 128), [(2 * planes, 2, 16, 128)])(u, v, after)
    far = lax.ppermute(edge, "gx", pairs("gx", 1))
    near = lax.ppermute(edge, "gx", pairs("gx", 0))
    padded = (2, planes, 16, rows)
    mid = call(inner_kernel, pltpu.VMEM(padded, f32), [padded])(u, v, after, edge)
    un, vn, back, send = call(
        step_kernel, (inside, inside, shape(2, planes, 2, rows), shape(128, 128)),
        [padded, (2, 256, 128), (rows, 128)],
    )(mid, edge, near, far)
    back = lax.ppermute(back, "gy", ring("gy", 1))
    un, vn = call(join_kernel, (brick, brick))(un, vn, back)
    order = [(i + master) % owners for i in range(owners)]
    got = lax.all_to_all(
        send.reshape(owners, 2, 128), "gy", 0, 0, tiled=True, axis_index_groups=[order]
    )
    out = call(
        rebuild_kernel, shape(32, 16, 128), [(512, 128), (2, 256, 128)], [(2,)],
        out_specs=pl.BlockSpec(memory_space=pl.ANY),
    )(got.reshape(128, 128))
    out = out.reshape(2, planes, 4, 4, 128).transpose(0, 1, 3, 2, 4).reshape(2, planes, 4, 512)
    return un, vn, out


def solution(mesh):
    in_specs = (P(None, "gy", "gx"), P(None, "gy", "gx"))
    out_specs = (P(None, "gy", "gx"), P(None, "gy", "gx"), P(None, None, ("gx", "gy"), None))
    return jax.shard_map(body, mesh=mesh, in_specs=in_specs, out_specs=out_specs, check_vma=False)
```

```python
import jax
import jax.numpy as jnp
from jax import lax
from jax.experimental import pallas as pl
from jax.experimental.pallas import tpu as pltpu
from jax.sharding import PartitionSpec as P

feed_rate = 0.037
kill_rate = 0.06
substrate_diffusion = 0.15
catalyst_diffusion = 0.08

planes, cols, rows = 16, 8, 256
owners = 64
large = 56 * 1024 * 1024
master = 47
f32 = jnp.float32


def lane_ids(shape):
    return lax.broadcasted_iota(jnp.int32, shape, len(shape) - 1)


def odd(axis):
    return lax.axis_index(axis) % 2 == 1


def slice_kernel(u_hbm, v_hbm, first_ref, u_ref, v_ref, sems):
    part, some = planes // 2, pl.ds(0, 4)
    copies = []
    for f, (src, dst) in enumerate(((u_hbm, u_ref), (v_hbm, v_ref))):
        for h in range(2):
            at = pl.ds(h * part, part)
            copy = pltpu.make_async_copy(src.at[at, some], dst.at[at, some], sems.at[f, h])
            copy.start()
            copies.append((f, h, copy))
    for f, h, copy in copies:
        copy.wait()
        at = slice(h * part, h * part + part)
        first_ref[f, at] = (u_ref, v_ref)[f][at, 0:4, :]


def fetch_kernel(u_hbm, v_hbm, first_ref, u_ref, v_ref, sems):
    del first_ref
    copies = [
        pltpu.make_async_copy(src, dst, sems.at[f])
        for f, (src, dst) in enumerate(((u_hbm, u_ref), (v_hbm, v_ref)))
    ]
    for copy in copies:
        copy.start()
    for copy in copies:
        copy.wait()


def edge_kernel(u_ref, v_ref, next_ref, edge_ref, pad_ref):
    lane = lane_ids((16, 128))
    low = lane < 64
    here = (lane < 2) | (lane >= 126)
    packed = jnp.zeros((16, 128), f32)
    for f, ref in enumerate((u_ref, v_ref)):
        for p in range(planes):
            q = f * planes + p
            for t, lanes in enumerate((slice(0, 128), slice(rows - 128, rows))):
                pad_ref[q, t, 0:6, :] = ref[p, 2:8, lanes]
                pad_ref[q, t, 6:10, :] = next_ref[f, p, :, lanes]
                pad_ref[q, t, 14:16, :] = ref[p, 0:2, lanes]
    for q in range(2 * planes):
        both = jnp.where(low, pad_ref[q, 0], pad_ref[q, 1])
        moved = pltpu.roll(jnp.where(here, both, 0.0), 4 * q % 128, 1)
        packed = packed + moved
    row = lax.broadcasted_iota(jnp.int32, (16, 128), 0)
    edge_ref[...] = jnp.where((row < 10) | (row >= 14), packed, 0.0)


def react(u, v, spread_u, spread_v):
    reaction = u * v * v
    new_u = u + substrate_diffusion * spread_u - reaction + feed_rate * (1.0 - u)
    new_v = v + catalyst_diffusion * spread_v + reaction - (feed_rate + kill_rate) * v
    return new_u, new_v


def inner_kernel(u_ref, v_ref, next_ref, edge_ref, mid_ref, pad_ref):
    del edge_ref
    for f, ref in enumerate((u_ref, v_ref)):
        pad_ref[f, :, 10:14, :] = jnp.zeros((planes, 4, rows), f32)
        pad_ref[f, :, 0:6, :] = ref[:, 2:8, :]
        pad_ref[f, :, 6:10, :] = next_ref[f]
        pad_ref[f, :, 14:16, :] = ref[:, 0:2, :]
    lane = lane_ids((16, rows))
    for p in range(planes):
        spreads = []
        for f in range(2):
            x = pad_ref[f, p]
            total = pad_ref[f, (p - 1) % planes] + pad_ref[f, (p + 1) % planes]
            total = total + pltpu.roll(x, 1, 0) + pltpu.roll(x, 15, 0)
            total = total + jnp.where(lane == 0, 0.0, pltpu.roll(x, 1, 1))
            total = total + jnp.where(lane == rows - 1, 0.0, pltpu.roll(x, rows - 1, 1))
            spreads.append(total - 6.0 * x)
        mid_ref[0, p], mid_ref[1, p] = react(pad_ref[0, p], pad_ref[1, p], *spreads)


def step_kernel(
    mid_ref, edge_ref, near_ref, far_ref,
    un_ref, vn_ref, back_ref, send_ref, full_ref, done_ref, turn_ref,
):
    lane = lane_ids((16, 128))
    edge = edge_ref[...]
    beside = jnp.where((lane % 4 < 2) != odd("gx"), near_ref[...], far_ref[...])

    place = (lane + 2) % 64
    total = jnp.where(place < 4, pltpu.roll(beside, 68, 1), pltpu.roll(beside, 4, 1))
    total = total + jnp.where(place >= 60, pltpu.roll(beside, 60, 1), pltpu.roll(beside, 124, 1))
    total = total + pltpu.roll(beside, 1, 0) + pltpu.roll(beside, 15, 0)
    total = total + jnp.where(
        lane % 4 == 3,
        pltpu.roll(beside, 1, 1) + pltpu.roll(edge, 127, 1),
        pltpu.roll(edge, 1, 1) + pltpu.roll(beside, 127, 1),
    )
    spread = total - 6.0 * beside
    other = pltpu.roll(beside, 64, 1)
    first = (lane + 2) % 128 < 64
    outer = react(jnp.where(first, beside, other), jnp.where(first, other, beside), spread, spread)
    outer = jnp.where(first, *outer)

    def swap(x):
        return jnp.where(lane_ids(x.shape) % 4 == 0, pltpu.roll(x, 1, 1), pltpu.roll(x, 127, 1))

    beside = swap(beside)
    for f, rate in enumerate((substrate_diffusion, catalyst_diffusion)):
        for p in range(planes):
            q = f * planes + p
            ends = pltpu.roll(beside, -4 * q % 128, 1)
            left = jnp.where(lane == 0, ends, 0.0)
            right = jnp.where(lane == 127, ends, 0.0)
            full_ref[f, p, :, 0:128] = mid_ref[f, p, :, 0:128] + rate * left
            full_ref[f, p, :, 128:256] = mid_ref[f, p, :, 128:256] + rate * right

    outer = swap(outer[0:8])
    lane = lane_ids((8, rows))
    for p in range(planes):
        spreads = []
        for f in range(2):
            q = f * planes + p
            x = full_ref[f, p]
            total = full_ref[f, (p - 1) % planes, 0:8, :] + full_ref[f, (p + 1) % planes, 0:8, :]
            total = total + pltpu.roll(x, 1, 0)[0:8] + pltpu.roll(x, 15, 0)[0:8]
            x = x[0:8]
            ends = pltpu.roll(outer, -4 * q % 128, 1)
            ends = jnp.concatenate([ends, ends], axis=1)
            total = total + jnp.where(lane == 0, ends, pltpu.roll(x, 1, 1))
            total = total + jnp.where(lane == rows - 1, ends, pltpu.roll(x, rows - 1, 1))
            spreads.append(total - 6.0 * x)
        news = react(full_ref[0, p, 0:8, :], full_ref[1, p, 0:8, :], *spreads)
        for f, (ref, new) in enumerate(zip((un_ref, vn_ref), news)):
            ref[p] = new
            back_ref[f, p] = new[6:8]
            at = 8 * (f * planes + p)
            for t in range(2):
                done_ref[t, at : at + 8, :] = new[:, 128 * t : 128 * t + 128]

    many = 2 * planes
    for t in range(2):
        pairs = []
        for c in range(cols // 2):
            one = done_ref[t, pl.ds(2 * c, many, stride=8), :]
            two = done_ref[t, pl.ds(2 * c + 1, many, stride=8), :]
            pairs.append(one + two)
        turn_ref[128 * t : 128 * t + 128, :] = jnp.concatenate(pairs, axis=0).T
    lane = lane_ids((owners, 128))
    r0 = 0.25 * (turn_ref[pl.ds(0, owners, stride=4), :] + turn_ref[pl.ds(1, owners, stride=4), :])
    r1 = 0.25 * (turn_ref[pl.ds(2, owners, stride=4), :] + turn_ref[pl.ds(3, owners, stride=4), :])
    for c1, out in enumerate((
        jnp.where(lane < 64, r0, pltpu.roll(r1, 64, 1)),
        jnp.where(lane < 64, pltpu.roll(r0, 64, 1), r1),
    )):
        turn_ref[c1 * owners : c1 * owners + owners, :] = out
    rest = owners - master
    for c1 in range(2):
        at = c1 * owners
        send_ref[pl.ds(c1, rest, stride=2), :] = turn_ref[at + master : at + owners, :]
        send_ref[pl.ds(2 * rest + c1, master, stride=2), :] = turn_ref[at : at + master, :]


def join_kernel(un_ref, vn_ref, back_ref, u_out, v_out):
    for f, (ref, out) in enumerate(((un_ref, u_out), (vn_ref, v_out))):
        out[:, 0:2, :] = back_ref[f]
        out[:, 2:8, :] = ref[:, 0:6, :]


def rebuild_kernel(got_ref, out_hbm, wide_ref, out_ref, sems):
    got = pltpu.roll(got_ref[...], 2 * master, 0)
    even = lane_ids((128, 128)) % 64 < 32
    level1 = jnp.where(even, pltpu.roll(pltpu.roll(got, 1, 0), 96, 1), pltpu.roll(got, 32, 1))
    total = level1 + pltpu.roll(level1, 64, 1)
    coarse = 0.25 * (total + pltpu.roll(total, 32, 1))
    blend = coarse + 0.5 * (level1 - coarse)
    shifted = pltpu.roll(blend, 96, 1)
    for d in range(2):
        wide_ref[pl.ds(d, 128, stride=4), :] = blend
        wide_ref[pl.ds(2 + d, 128, stride=4), :] = shifted
    copies = []
    for half in range(2):
        for t in range(2):
            at = 128 * (2 * half + t)
            turned = wide_ref[at : at + 128, :].T
            for r in range(2):
                part = turned[64 * r : 64 * r + 32]
                for d in range(2):
                    out_ref[half, pl.ds(4 * t + 2 * r + d, 32, stride=8), :] = part
        copies.append(pltpu.make_async_copy(
            out_ref.at[half].reshape(32, 8, 128), out_hbm.at[:, pl.ds(8 * half, 8), :], sems.at[half]
        ))
        copies[-1].start()
    for copy in copies:
        copy.wait()


def call(kernel, out_shape, scratch=(), sems=(), limit=32 * 1024 * 1024, **kw):
    return pl.pallas_call(
        kernel,
        out_shape=out_shape,
        scratch_shapes=[pltpu.VMEM(s, f32) for s in scratch] + [pltpu.SemaphoreType.DMA(s) for s in sems],
        compiler_params=pltpu.CompilerParams(vmem_limit_bytes=limit),
        **kw,
    )


def shape(*dims):
    return jax.ShapeDtypeStruct(dims, f32)


def ring(axis, by):
    size = lax.axis_size(axis)
    return [(i, (i + by) % size) for i in range(size)]


def pairs(axis, first):
    size = lax.axis_size(axis)
    found = [(i % size, (i + 1) % size) for i in range(first, size, 2)]
    return found + [(j, i) for i, j in found]


def body(u, v):
    brick = shape(planes, cols, rows)
    inside = pltpu.VMEM((planes, cols, rows), f32)
    first = call(
        slice_kernel, pltpu.VMEM((2, planes, 4, rows), f32), [(planes, cols, rows)] * 2, [(2, 2)],
        limit=large, in_specs=[pl.BlockSpec(memory_space=pltpu.HBM)] * 2,
    )(u, v)
    after = lax.ppermute(first, "gy", ring("gy", -1))
    u, v = call(
        fetch_kernel, (inside, inside), sems=[(2,)], limit=large,
        in_specs=[pl.BlockSpec(memory_space=pltpu.HBM)] * 2 + [pl.BlockSpec(memory_space=pl.ANY)],
    )(u, v, first)
    edge = call(edge_kernel, shape(16, 128), [(2 * planes, 2, 16, 128)])(u, v, after)
    far = lax.ppermute(edge, "gx", pairs("gx", 1))
    near = lax.ppermute(edge, "gx", pairs("gx", 0))
    padded = (2, planes, 16, rows)
    mid = call(inner_kernel, pltpu.VMEM(padded, f32), [padded])(u, v, after, edge)
    un, vn, back, send = call(
        step_kernel, (inside, inside, shape(2, planes, 2, rows), shape(128, 128)),
        [padded, (2, 256, 128), (rows, 128)],
    )(mid, edge, near, far)
    back = lax.ppermute(back, "gy", ring("gy", 1))
    un, vn = call(join_kernel, (brick, brick))(un, vn, back)
    order = [(i + master) % owners for i in range(owners)]
    got = lax.all_to_all(
        send.reshape(owners, 2, 128), "gy", 0, 0, tiled=True, axis_index_groups=[order]
    )
    out = call(
        rebuild_kernel, shape(32, 16, 128), [(512, 128), (2, 256, 128)], [(2,)],
        out_specs=pl.BlockSpec(memory_space=pl.ANY),
    )(got.reshape(128, 128))
    out = out.reshape(2, planes, 4, 4, 128).transpose(0, 1, 3, 2, 4).reshape(2, planes, 4, 512)
    return un, vn, out


def solution(mesh):
    in_specs = (P(None, "gy", "gx"), P(None, "gy", "gx"))
    out_specs = (P(None, "gy", "gx"), P(None, "gy", "gx"), P(None, None, ("gx", "gy"), None))
    return jax.shard_map(body, mesh=mesh, in_specs=in_specs, out_specs=out_specs, check_vma=False)
```
